256 devices in a mesh: req: 4 (over x_lo, core), ctx: 64 (over x_hi, z, y).
Axes of the slice: x: 4 (x_hi: 2, x_lo: 2; x = x_hi * 2 + x_lo), y: 4, z: 8, core: 2. Of those that a mesh axis runs over, the one named last changes fastest.
Arguments:
- queries: bfloat16 [4, 64, 64, 6144], P('req', 'ctx'), may hold values from -160 to 160, as said below
- keys: bfloat16 [4, 32768, 128], P('req', 'ctx'), may hold values from -6 to 6
- values: bfloat16 [4, 32768, 128], P('req', 'ctx'), may hold values from -6 to 6
- query_host: int32 [4], P('req'), may hold values from 0 to 63
- lengths: int32 [4, 64], P('req', 'ctx'), may hold values from 1 to 4, as said below
Outputs:
- attended: bfloat16 [4, 64, 6144], P('req')
- log_total: float32 [4, 64, 48], P('req', 'ctx')
The draws below stay inside these ranges and needn't reach their ends.
Inputs may be any that keep to these rules, and one draw needn't show every extreme that they name: Each request's queries; every entry within the range. `lengths`: number of leading valid 128-token blocks in a device's slots; every device has at least one, and in every request some device is full (4) and some device has exactly one.
All inputs are finite; a program needn't handle non-finite values.
Results may differ from the reference program's by a relative error of at most 0.0044.
Values may be sent and summed in bfloat16 or wider, within the bound.
A program may use at most 256 MiB of HBM per device.

```python
import jax
import jax.numpy as jnp
from jax import lax

H = 48
DH = 128
QTOK = 64
CTX_DEV = 512
BLOCK = 128
REQ = 4
CONTEXT = 32768
HD = 6144
N_CTX = 64


def shared_base(key):
    return jnp.clip(jax.random.normal(key, (REQ, CONTEXT, DH), jnp.float32), -6.0, 6.0)


def draw_keys(key, part):
    base = shared_base(key)
    return base.astype(jnp.bfloat16)


def draw_queries(key, part):
    key = jax.random.fold_in(key, 5)
    drawn = jnp.clip(jax.random.normal(key, (REQ, N_CTX, QTOK, H * DH), jnp.float32), -6.0, 6.0)
    return drawn.astype(jnp.bfloat16)


def draw_lengths(key, part):
    key = jax.random.fold_in(key, 7)
    first, second, third = jax.random.split(key, 3)
    most = CTX_DEV // 128
    drawn = jax.random.randint(first, (REQ, N_CTX), 1, most + 1)
    full_at = jax.random.randint(second, (REQ, 1), 0, N_CTX)
    one_at = (full_at + 1 + jax.random.randint(third, (REQ, 1), 0, N_CTX - 1)) % N_CTX
    slots = jnp.arange(N_CTX, dtype=jnp.int32)[None, :]
    drawn = jnp.where(slots == full_at, most, drawn)
    drawn = jnp.where(slots == one_at, 1, drawn)
    return drawn.astype(jnp.int32)


def set_ends(entries, rng, smallest, largest):
    spot = [jax.random.randint(jax.random.fold_in(rng, axis), (), 0, length) for axis, length in enumerate(entries.shape)]
    main_axis = entries.shape.index(max(entries.shape))
    next_to = spot[:main_axis] + [(spot[main_axis] + 1) % entries.shape[main_axis]] + spot[main_axis + 1:]
    return entries.at[tuple(spot)].set(smallest).at[tuple(next_to)].set(largest)


def levels(own_key, extent, shards, low, high):
    loudness, own = 1.0, jax.random.fold_in(own_key, 6)
    for position, shards_of in shards:
        draws = jnp.exp(jax.random.uniform(jax.random.fold_in(own, position), (shards_of,), jnp.float32, low / len(shards), high / len(shards)))
        loudness = loudness * jnp.repeat(draws, extent[position] // shards_of).reshape([-1 if axis == position else 1 for axis in range(len(extent))])
    return loudness


def gaussian(stream_key, extent, spread, limit, cuts=(), kind=jnp.bfloat16):
    array = spread * jax.random.normal(stream_key, extent, jnp.float32)
    if cuts:
        array = array * levels(stream_key, extent, cuts, -0.22, 0.18)
    return jnp.clip(array, -limit, limit).astype(kind)


def setup_inputs(seed: int = 0) -> dict:
    seeds = jax.random.split(jax.random.key(seed), 6)
    queries = draw_queries(jax.random.fold_in(seeds[5], 71), 0)
    keys = draw_keys(jax.random.fold_in(seeds[5], 71), 0)
    values = gaussian(seeds[2], (REQ, CONTEXT, DH), 1.0, 6.0, ((0, 4), (1, 64)))
    query_host = set_ends(jax.random.randint(seeds[3], (REQ,), 0, N_CTX), jax.random.fold_in(seeds[3], 1), 0, N_CTX - 1).astype(jnp.int32)
    lengths = draw_lengths(jax.random.fold_in(seeds[5], 71), 0)
    return {"queries": queries, "keys": keys, "values": values, "query_host": query_host, "lengths": lengths}


NEG = -1e30


def one_request(operands):
    query_all, key_all, value_all, host, lens = operands
    per_dev = CTX_DEV // BLOCK
    query_matrix = lax.dynamic_index_in_dim(query_all, host, 0, keepdims=False)
    query_matrix = query_matrix.reshape(QTOK, H, DH).astype(jnp.float32)
    key_blocks = key_all.reshape(CONTEXT // BLOCK, BLOCK, DH).astype(jnp.float32)
    value_blocks = value_all.reshape(CONTEXT // BLOCK, BLOCK, DH).astype(jnp.float32)
    block_ids = jnp.arange(CONTEXT // BLOCK, dtype=jnp.int32)
    valid = ((block_ids % per_dev) < jnp.repeat(lens, per_dev)).astype(jnp.float32)
    softmax_scale = float(DH) ** -0.5

    def step(carry, item):
        top, total, numer = carry
        key_block_slice, value_block_slice, ok = item
        logit_scores = jnp.einsum('qhd,kd->qhk', query_matrix, key_block_slice) * softmax_scale
        block_max = jnp.max(logit_scores, axis=-1)
        expo = jnp.exp(logit_scores - block_max[..., None])
        block_total = jnp.sum(expo, axis=-1)
        attention_weights = lax.optimization_barrier(expo.astype(jnp.bfloat16)).astype(jnp.float32)
        block_result = jnp.einsum('qhk,kd->qhd', attention_weights, value_block_slice)
        block_max = jnp.where(ok > 0, block_max, NEG)
        new_top = jnp.maximum(top, block_max)
        keep = jnp.exp(top - new_top)
        factor = jnp.exp(block_max - new_top) * ok
        total = total * keep + block_total * factor
        numer = numer * keep[..., None] + block_result * factor[..., None]
        return (new_top, total, numer), None

    start = (jnp.full((QTOK, H), NEG, jnp.float32), jnp.zeros((QTOK, H), jnp.float32), jnp.zeros((QTOK, H, DH), jnp.float32))
    (top, total, numer), _ = lax.scan(step, start, (key_blocks, value_blocks, valid))
    attended = (numer / total[..., None]).astype(jnp.bfloat16).reshape(QTOK, HD)
    return attended, top + jnp.log(total)


def reference(queries, keys, values, query_host, lengths):
    return lax.map(one_request, (queries, keys, values, query_host.astype(jnp.int32), lengths.astype(jnp.int32)))
```

```python
import math

import jax
import jax.numpy as jnp
from jax import lax
from jax.experimental import pallas as pl
from jax.experimental.pallas import tpu as pltpu
from jax.sharding import PartitionSpec as P


H = 48
DH = 128
T = 64
KEYS = 512
BLOCK = 128
HD = H * DH
NZ = 8
NXY = 8
ROWS = 384
PIECE = 48
A_COLS = 4096
NEG = -1e30
LOG2E = math.log2(math.e)
LN2 = math.log(2.0)
SCALE = DH ** -0.5 * LOG2E
MESH = pl.DeviceIdType.MESH


def kernel(host_ref, len_ref, q_ref, k_ref, v_ref, out_ref, log_ref,
           kv, s1a, s1b, x2a, x2b, s2a, s2b, qg, qm, acc, top, po, ps, o_in, st_in, lg,
           loc_sem, kv_send, kv_recv, send, recv):
    me = lax.axis_index("ctx")
    x, z, y = me // 32, (me // 4) % 8, me % 4
    xy = x * 4 + y
    tg, hg = z // 2, z % 2

    def z_of(k):
        return lax.rem(z + k, NZ)

    def at_z(zz):
        return {"ctx": x * 32 + zz * 4 + y}

    def xy_to(k):
        px, py = lax.rem(x + k // 4, 2), lax.rem(y + k % 4, 4)
        return px * 4 + py, {"ctx": px * 32 + z * 4 + py}

    def put(src, dst, stage, device):
        pltpu.make_async_remote_copy(
            src_ref=src, dst_ref=dst, send_sem=send.at[stage], recv_sem=recv.at[stage],
            device_id=device, device_id_type=MESH).start()

    def both(stage, like):
        return pltpu.make_async_remote_copy(
            src_ref=like, dst_ref=like, send_sem=send.at[stage], recv_sem=recv.at[stage],
            device_id=at_z(z_of(1)), device_id_type=MESH)

    def cols(start, n):
        return pl.ds(pl.multiple_of(start, 128), n)

    def rows(start, n):
        return pl.ds(pl.multiple_of(start, 16), n)

    z_order = (4, 3, 5, 2, 6, 1, 7)
    xy_order = (6, 5, 7, 2, 4, 1, 3)

    def a_chunk(c):
        return q_ref.at[:, cols(c * 512, 512)]

    def b_chunk(zz):
        return q_ref.at[rows((zz // 2) * 16, 16), cols(A_COLS + lax.rem(zz, 2) * 1024, 1024)]

    local = [
        pltpu.make_async_copy(k_ref, kv.at[xy, pl.ds(0, KEYS)], loc_sem.at[0]),
        pltpu.make_async_copy(v_ref, kv.at[xy, pl.ds(KEYS, KEYS)], loc_sem.at[1]),
        pltpu.make_async_copy(a_chunk(xy), s1a.at[xy], loc_sem.at[2]),
        pltpu.make_async_copy(b_chunk(z), s1b.at[z], loc_sem.at[3]),
    ]
    for copy in local:
        copy.start()

    barrier = pltpu.get_barrier_semaphore()
    for k in range(1, NZ):
        pl.semaphore_signal(barrier, inc=1, device_id=at_z(z_of(k)), device_id_type=MESH)
    for k in range(1, NXY):
        pl.semaphore_signal(barrier, inc=1, device_id=xy_to(k)[1], device_id_type=MESH)
    length = len_ref[0, 0].astype(jnp.float32)
    kv[xy, 2 * KEYS:, :] = jnp.full((16, DH), length, jnp.float32).astype(jnp.bfloat16)
    pl.semaphore_wait(barrier, 14)

    for k in xy_order:
        c, device = xy_to(k)
        put(a_chunk(c), s1a.at[xy], 0, device)
    for k in z_order:
        zz = z_of(k)
        put(b_chunk(zz), s1b.at[z], 1, at_z(zz))
    local[0].wait()
    local[1].wait()

    def kv_copy(k):
        return pltpu.make_async_remote_copy(
            src_ref=kv.at[xy], dst_ref=kv.at[xy], send_sem=kv_send.at[k], recv_sem=kv_recv.at[k],
            device_id=xy_to(k)[1], device_id_type=MESH)

    for k in range(1, NXY):
        kv_copy(k).start()

    host = host_ref[0]
    host_z = lax.rem(host // 4, 8)
    host_xy = host // 32 * 4 + lax.rem(host, 4)

    local[2].wait()
    both(0, s1a.at[pl.ds(0, 7)]).wait_recv()
    chunk = s1a[host_xy]
    for p in range(NZ):
        a, b = p // 2, p % 2
        x2a[p] = chunk[16 * a:16 * a + 16, 256 * b:256 * b + 256]
    s2a[z] = x2a[z]
    for k in z_order:
        zz = z_of(k)
        put(x2a.at[zz], s2a.at[z], 2, at_z(zz))
    local[3].wait()
    both(1, s1b.at[pl.ds(0, 7)]).wait_recv()
    chunk = s1b[host_z]
    for p in range(NXY):
        x2b[p] = chunk[:, 128 * p:128 * p + 128]
    s2b[xy] = x2b[xy]
    for k in xy_order:
        c, device = xy_to(k)
        put(x2b.at[c], s2b.at[xy], 3, device)

    both(2, s2a.at[pl.ds(0, 7)]).wait_recv()
    both(3, s2b.at[pl.ds(0, 7)]).wait_recv()
    qg[z, :, 0:256] = s2a[host_z]
    qg[z, :, 256:384] = s2b[host_xy]
    for k in z_order:
        put(qg.at[z], qg.at[z], 4, at_z(z_of(k)))
    both(4, qg.at[pl.ds(0, 7)]).wait_recv()
    for p in range(NZ):
        for c in range(3):
            qm[PIECE * p + 16 * c:PIECE * p + 16 * c + 16, :] = qg[p, :, 128 * c:128 * c + 128]

    acc[...] = jnp.zeros_like(acc)
    top[...] = jnp.full(top.shape, NEG, jnp.float32)
    block_id = lax.broadcasted_iota(jnp.int32, (1, KEYS), 1) // BLOCK

    def attend(c):
        valid = kv[c, 2 * KEYS:2 * KEYS + 16, :].astype(jnp.float32)[0:1, :]
        valid = jnp.concatenate([valid] * (KEYS // DH), axis=1)
        score = lax.dot_general(
            qm[...], kv[c, 0:KEYS, :], (((1,), (1,)), ((), ())), preferred_element_type=jnp.float32)
        score = jnp.where(block_id.astype(jnp.float32) < valid, score * SCALE, NEG)
        old = top[:, 0:1]
        new = jnp.maximum(old, jnp.max(score, axis=1, keepdims=True))
        weight = jnp.exp2(score - new).astype(jnp.bfloat16)
        value = jnp.concatenate(
            [kv[c, KEYS:2 * KEYS, :], jnp.ones((KEYS, DH), jnp.bfloat16)], axis=1)
        acc[...] = acc[...] * jnp.exp2(old - new) + jnp.dot(
            weight, value, preferred_element_type=jnp.float32)
        top[...] = jnp.broadcast_to(new, top.shape)

    attend(xy)

    def step(k, carry):
        c = lax.rem(x + k // 4, 2) * 4 + lax.rem(y - lax.rem(k, 4) + 4, 4)
        pltpu.make_async_remote_copy(
            src_ref=kv.at[c], dst_ref=kv.at[c], send_sem=kv_send.at[k], recv_sem=kv_recv.at[k],
            device_id=at_z(z_of(1)), device_id_type=MESH).wait_recv()
        attend(c)
        return carry

    lax.fori_loop(1, NXY, step, 0)

    total = acc[:, DH:]
    po[...] = (acc[:, :DH] / total).astype(jnp.bfloat16).reshape(NZ, PIECE, DH)
    lse = top[...] + jnp.log(total) * LOG2E
    lane = lax.broadcasted_iota(jnp.int32, (PIECE, DH), 1)
    diagonal = lane == lax.broadcasted_iota(jnp.int32, (PIECE, DH), 0)
    for p in range(NZ):
        part = lse[PIECE * p:PIECE * p + PIECE, :]
        ps[p] = jnp.sum(jnp.where(diagonal, part, 0.0), axis=0, keepdims=True)
    o_in[z] = po[z]
    st_in[z] = ps[z]
    for k in z_order:
        zz = z_of(k)
        put(po.at[zz], o_in.at[z], 5, at_z(zz))
        put(ps.at[zz], st_in.at[z], 6, at_z(zz))
    both(6, st_in.at[pl.ds(0, 7)]).wait_recv()
    stat = jnp.concatenate([st_in[s] for s in range(NZ)], axis=0)
    overall = jnp.max(stat, axis=0, keepdims=True)
    share = jnp.exp2(stat - overall)
    summed = jnp.sum(share, axis=0, keepdims=True)
    share = share / summed
    lg[xy, z] = overall * LN2 + jnp.log(summed)
    both(5, o_in.at[pl.ds(0, 7)]).wait_recv()
    result = jnp.zeros((PIECE, DH), jnp.float32)
    for s in range(NZ):
        column = jnp.sum(jnp.where(diagonal, share[s:s + 1, :], 0.0), axis=1, keepdims=True)
        result = result + column * o_in[s].astype(jnp.float32)
    result = result.astype(jnp.bfloat16)

    mine = rows(tg * 16, 16)
    a_here = out_ref.at[mine, cols(xy * 512 + hg * 256, 256)]
    b_here = out_ref.at[mine, cols(A_COLS + hg * 1024 + xy * 128, 128)]
    out_ref[mine, cols(xy * 512 + hg * 256, 128)] = result[0:16]
    out_ref[mine, cols(xy * 512 + hg * 256 + 128, 128)] = result[16:32]
    out_ref[mine, cols(A_COLS + hg * 1024 + xy * 128, 128)] = result[32:48]
    for k in z_order:
        put(a_here, a_here, 7, at_z(z_of(k)))
    for k in xy_order:
        put(b_here, b_here, 8, xy_to(k)[1])
    for k in z_order:
        put(lg.at[xy, z], lg.at[xy, z], 9, at_z(z_of(k)))
    both(7, s2a.at[pl.ds(0, 7)]).wait_recv()
    a_all = out_ref.at[:, cols(xy * 512, 512)]
    for k in xy_order:
        put(a_all, a_all, 10, xy_to(k)[1])
    both(8, s2b.at[pl.ds(0, 7)]).wait_recv()
    b_all = out_ref.at[mine, cols(A_COLS + hg * 1024, 1024)]
    for k in z_order:
        put(b_all, b_all, 11, at_z(z_of(k)))
    both(9, st_in.at[pl.ds(0, 7)]).wait_recv()
    for k in xy_order:
        put(lg.at[xy], lg.at[xy], 12, xy_to(k)[1])

    both(12, lg.at[pl.ds(0, 7)]).wait_recv()
    t_group, t_in = me // 16, lax.rem(me, 16)
    lane = lax.broadcasted_iota(jnp.int32, (NXY, DH), 1)
    source = lax.broadcasted_iota(jnp.int32, (NXY, DH), 0)
    logs = jnp.zeros((NXY, DH), jnp.float32)
    for b in range(2):
        part = jnp.concatenate([lg[c, 2 * t_group + b] for c in range(NXY)], axis=0)
        for c in range(3):
            column = jnp.sum(jnp.where(lane == 16 * c + t_in, part, 0.0), axis=1, keepdims=True)
            head = source * 4 + 2 * b + c if c < 2 else 32 + 8 * b + source
            logs = logs + jnp.where(lane == head, column, 0.0)
    log_ref[...] = jnp.sum(logs, axis=0, keepdims=True)[:, :H]

    both(10, s1a.at[pl.ds(0, 7)]).wait_recv()
    both(11, s1b.at[pl.ds(0, 7)]).wait_recv()
    for stage, like in enumerate((s1a, s1b, s2a, s2b, qg, o_in, st_in, s2a, s2b, st_in, s1a, s1b, lg)):
        both(stage, like.at[pl.ds(0, 7)]).wait_send()
    for k in range(1, NXY):
        kv_copy(k).wait_send()


def body(queries, keys, values, query_host, lengths):
    bf16, f32 = jnp.bfloat16, jnp.float32
    attended, log_total = pl.pallas_call(
        kernel,
        out_shape=(
            jax.ShapeDtypeStruct((T, HD), bf16),
            jax.ShapeDtypeStruct((1, H), f32),
        ),
        in_specs=[
            pl.BlockSpec(memory_space=pltpu.SMEM),
            pl.BlockSpec(memory_space=pltpu.SMEM),
            pl.BlockSpec(memory_space=pl.ANY),
            pl.BlockSpec(memory_space=pl.ANY),
            pl.BlockSpec(memory_space=pl.ANY),
        ],
        out_specs=(
            pl.BlockSpec(memory_space=pltpu.VMEM),
            pl.BlockSpec(memory_space=pltpu.VMEM),
        ),
        scratch_shapes=[
            pltpu.VMEM((NXY, 2 * KEYS + 16, DH), bf16),
            pltpu.VMEM((NXY, T, 512), bf16),
            pltpu.VMEM((NZ, 16, 1024), bf16),
            pltpu.VMEM((NZ, 16, 256), bf16),
            pltpu.VMEM((NXY, 16, 128), bf16),
            pltpu.VMEM((NZ, 16, 256), bf16),
            pltpu.VMEM((NXY, 16, 128), bf16),
            pltpu.VMEM((NZ, 16, 384), bf16),
            pltpu.VMEM((ROWS, DH), bf16),
            pltpu.VMEM((ROWS, 2 * DH), f32),
            pltpu.VMEM((ROWS, DH), f32),
            pltpu.VMEM((NZ, PIECE, DH), bf16),
            pltpu.VMEM((NZ, 1, DH), f32),
            pltpu.VMEM((NZ, PIECE, DH), bf16),
            pltpu.VMEM((NZ, 1, DH), f32),
            pltpu.VMEM((NXY, NZ, 1, DH), f32),
            pltpu.SemaphoreType.DMA((4,)),
            pltpu.SemaphoreType.DMA((NXY,)),
            pltpu.SemaphoreType.DMA((NXY,)),
            pltpu.SemaphoreType.DMA((13,)),
            pltpu.SemaphoreType.DMA((13,)),
        ],
        compiler_params=pltpu.CompilerParams(
            collective_id=0, has_side_effects=True, vmem_limit_bytes=40 * 2**20),
    )(query_host, lengths, queries.reshape(T, HD), keys.reshape(KEYS, DH), values.reshape(KEYS, DH))
    return attended[None], log_total[None]


def solution(mesh):
    return jax.shard_map(
        body,
        mesh=mesh,
        in_specs=(
            P("req", "ctx", None, None),
            P("req", "ctx", None),
            P("req", "ctx", None),
            P("req"),
            P("req", "ctx"),
        ),
        out_specs=(P("req", None, None), P("req", "ctx", None)),
        check_vma=False,
    )
```

```python
import math

import jax
import jax.numpy as jnp
from jax import lax
from jax.experimental import pallas as pl
from jax.experimental.pallas import tpu as pltpu
from jax.sharding import PartitionSpec as P


H = 48
DH = 128
T = 64
KEYS = 512
BLOCK = 128
HD = H * DH
NZ = 8
NXY = 8
ROWS = 384
PIECE = 48
A_COLS = 4096
NEG = -1e30
LOG2E = math.log2(math.e)
LN2 = math.log(2.0)
SCALE = DH ** -0.5 * LOG2E
MESH = pl.DeviceIdType.MESH


def kernel(host_in, len_in, q_ref, k_ref, v_ref, out_ref, log_ref,
           host_ref, len_ref, kv, s1a, s1b, x2a, x2b, s2a, s2b, qg, qm, acc, top, po, ps, o_in, st_in,
           oa, ob, lg, loc_sem, kv_send, kv_recv, send, recv):
    me = lax.axis_index("ctx")
    x, z, y = me // 32, (me // 4) % 8, me % 4
    xy = x * 4 + y
    tg, hg = z // 2, z % 2

    def z_of(k):
        return lax.rem(z + k, NZ)

    def at_z(zz):
        return {"ctx": x * 32 + zz * 4 + y}

    def xy_to(k):
        px, py = lax.rem(x + k // 4, 2), lax.rem(y + k % 4, 4)
        return px * 4 + py, {"ctx": px * 32 + z * 4 + py}

    def put(src, dst, stage, device):
        pltpu.make_async_remote_copy(
            src_ref=src, dst_ref=dst, send_sem=send.at[stage], recv_sem=recv.at[stage],
            device_id=device, device_id_type=MESH).start()

    def both(stage, like):
        return pltpu.make_async_remote_copy(
            src_ref=like, dst_ref=like, send_sem=send.at[stage], recv_sem=recv.at[stage],
            device_id=at_z(z_of(1)), device_id_type=MESH)

    def cols(start, n):
        return pl.ds(pl.multiple_of(start, 128), n)

    def rows(start, n):
        return pl.ds(pl.multiple_of(start, 16), n)

    z_order = (4, 3, 5, 2, 6, 1, 7)
    xy_order = (6, 5, 7, 2, 4, 1, 3)

    def a_chunk(c):
        return q_ref.at[:, cols(c * 512, 512)]

    def b_chunk(zz):
        return q_ref.at[rows((zz // 2) * 16, 16), cols(A_COLS + lax.rem(zz, 2) * 1024, 1024)]

    barrier = pltpu.get_barrier_semaphore()
    for k in range(1, NZ):
        pl.semaphore_signal(barrier, inc=1, device_id=at_z(z_of(k)), device_id_type=MESH)
    for k in range(1, NXY):
        pl.semaphore_signal(barrier, inc=1, device_id=xy_to(k)[1], device_id_type=MESH)
    local = [
        pltpu.make_async_copy(len_in, len_ref, loc_sem.at[4]),
        pltpu.make_async_copy(host_in, host_ref, loc_sem.at[5]),
        pltpu.make_async_copy(k_ref, kv.at[xy, pl.ds(0, KEYS)], loc_sem.at[0]),
        pltpu.make_async_copy(v_ref, kv.at[xy, pl.ds(KEYS, KEYS)], loc_sem.at[1]),
        pltpu.make_async_copy(a_chunk(xy), s1a.at[xy], loc_sem.at[2]),
        pltpu.make_async_copy(b_chunk(z), s1b.at[z], loc_sem.at[3]),
    ]
    for copy in local:
        copy.start()
    local[0].wait()
    length = len_ref[0, 0].astype(jnp.float32)
    kv[xy, 2 * KEYS:, :] = jnp.full((16, DH), length, jnp.float32).astype(jnp.bfloat16)
    local[1].wait()
    host = host_ref[0]
    host_z = lax.rem(host // 4, 8)
    host_xy = host // 32 * 4 + lax.rem(host, 4)
    pl.semaphore_wait(barrier, 14)

    for k in xy_order:
        c, device = xy_to(k)
        put(a_chunk(c), s1a.at[xy], 0, device)
    for k in z_order:
        zz = z_of(k)
        put(b_chunk(zz), s1b.at[z], 1, at_z(zz))
    local[2].wait()
    local[3].wait()
    up, down, over = lax.rem(y + 1, 4), lax.rem(y + 3, 4), 1 - x
    far = lax.rem(y + 2, 4)
    to_up = {"ctx": x * 32 + z * 4 + up}
    to_down = {"ctx": x * 32 + z * 4 + down}
    to_over = {"ctx": over * 32 + z * 4 + y}
    whole, k_half, v_half = (0, 2 * KEYS + 16), (0, KEYS), (KEYS, KEYS + 16)

    def kv_copy(slot, part, sem, device):
        ref = kv.at[slot, pl.ds(*part)]
        return pltpu.make_async_remote_copy(
            src_ref=ref, dst_ref=ref, send_sem=kv_send.at[sem], recv_sem=kv_recv.at[sem],
            device_id=device, device_id_type=MESH)

    kv_sent = [
        kv_copy(xy, whole, 0, to_over),
        kv_copy(xy, whole, 1, to_up),
        kv_copy(xy, whole, 2, to_down),
        kv_copy(over * 4 + y, whole, 3, to_up),
        kv_copy(over * 4 + y, whole, 4, to_down),
        kv_copy(x * 4 + down, k_half, 5, to_up),
        kv_copy(x * 4 + up, v_half, 6, to_down),
        kv_copy(over * 4 + down, k_half, 7, to_up),
        kv_copy(over * 4 + up, v_half, 8, to_down),
    ]
    kv_got = [
        kv_copy(over * 4 + y, whole, 0, to_over),
        kv_copy(x * 4 + down, whole, 1, to_up),
        kv_copy(x * 4 + up, whole, 2, to_down),
        kv_copy(over * 4 + down, whole, 3, to_up),
        kv_copy(over * 4 + up, whole, 4, to_down),
        kv_copy(x * 4 + far, k_half, 5, to_up),
        kv_copy(x * 4 + far, v_half, 6, to_down),
        kv_copy(over * 4 + far, k_half, 7, to_up),
        kv_copy(over * 4 + far, v_half, 8, to_down),
    ]
    for n in range(3):
        kv_sent[n].start()

    local[4].wait()
    both(0, s1a.at[pl.ds(0, 7)]).wait_recv()
    chunk = s1a[host_xy]
    for p in range(NZ):
        a, b = p // 2, p % 2
        x2a[p] = chunk[16 * a:16 * a + 16, 256 * b:256 * b + 256]
    s2a[z] = x2a[z]
    for k in z_order:
        zz = z_of(k)
        put(x2a.at[zz], s2a.at[z], 2, at_z(zz))
    local[5].wait()
    both(1, s1b.at[pl.ds(0, 7)]).wait_recv()
    chunk = s1b[host_z]
    for p in range(NXY):
        x2b[p] = chunk[:, 128 * p:128 * p + 128]
    s2b[xy] = x2b[xy]
    for k in xy_order:
        c, device = xy_to(k)
        put(x2b.at[c], s2b.at[xy], 3, device)

    kv_got[0].wait_recv()
    kv_sent[3].start()
    kv_sent[4].start()
    kv_got[1].wait_recv()
    kv_sent[5].start()
    kv_got[2].wait_recv()
    kv_sent[6].start()

    both(2, s2a.at[pl.ds(0, 7)]).wait_recv()
    both(3, s2b.at[pl.ds(0, 7)]).wait_recv()
    qg[z, :, 0:256] = s2a[host_z]
    qg[z, :, 256:384] = s2b[host_xy]
    for k in z_order:
        put(qg.at[z], qg.at[z], 4, at_z(z_of(k)))
    kv_got[3].wait_recv()
    kv_sent[7].start()
    kv_got[4].wait_recv()
    kv_sent[8].start()
    both(4, qg.at[pl.ds(0, 7)]).wait_recv()
    for p in range(NZ):
        for c in range(3):
            qm[PIECE * p + 16 * c:PIECE * p + 16 * c + 16, :] = qg[p, :, 128 * c:128 * c + 128]

    acc[...] = jnp.zeros_like(acc)
    top[...] = jnp.full(top.shape, NEG, jnp.float32)
    block_id = lax.broadcasted_iota(jnp.int32, (1, KEYS), 1) // BLOCK

    def attend(c):
        valid = kv[c, 2 * KEYS:2 * KEYS + 16, :].astype(jnp.float32)[0:1, :]
        valid = jnp.concatenate([valid] * (KEYS // DH), axis=1)
        score = lax.dot_general(
            qm[...], kv[c, 0:KEYS, :], (((1,), (1,)), ((), ())), preferred_element_type=jnp.float32)
        score = jnp.where(block_id.astype(jnp.float32) < valid, score * SCALE, NEG)
        old = top[:, 0:1]
        new = jnp.maximum(old, jnp.max(score, axis=1, keepdims=True))
        weight = jnp.exp2(score - new).astype(jnp.bfloat16)
        value = jnp.concatenate(
            [kv[c, KEYS:2 * KEYS, :], jnp.ones((KEYS, DH), jnp.bfloat16)], axis=1)
        acc[...] = acc[...] * jnp.exp2(old - new) + jnp.dot(
            weight, value, preferred_element_type=jnp.float32)
        top[...] = jnp.broadcast_to(new, top.shape)

    attend(xy)
    attend(over * 4 + y)
    attend(x * 4 + down)
    attend(x * 4 + up)
    attend(over * 4 + down)
    attend(over * 4 + up)
    kv_got[5].wait_recv()
    kv_got[6].wait_recv()
    attend(x * 4 + far)
    kv_got[7].wait_recv()
    kv_got[8].wait_recv()
    attend(over * 4 + far)

    total = acc[:, DH:]
    po[...] = (acc[:, :DH] / total).astype(jnp.bfloat16).reshape(NZ, PIECE, DH)
    lse = top[...] + jnp.log(total) * LOG2E
    lane = lax.broadcasted_iota(jnp.int32, (PIECE, DH), 1)
    diagonal = lane == lax.broadcasted_iota(jnp.int32, (PIECE, DH), 0)
    for p in range(NZ):
        part = lse[PIECE * p:PIECE * p + PIECE, :]
        ps[p] = jnp.sum(jnp.where(diagonal, part, 0.0), axis=0, keepdims=True)
    o_in[z] = po[z]
    st_in[z] = ps[z]
    for k in z_order:
        zz = z_of(k)
        put(po.at[zz], o_in.at[z], 5, at_z(zz))
        put(ps.at[zz], st_in.at[z], 6, at_z(zz))
    both(6, st_in.at[pl.ds(0, 7)]).wait_recv()
    stat = jnp.concatenate([st_in[s] for s in range(NZ)], axis=0)
    overall = jnp.max(stat, axis=0, keepdims=True)
    share = jnp.exp2(stat - overall)
    summed = jnp.sum(share, axis=0, keepdims=True)
    share = share / summed
    lg[xy, z] = overall * LN2 + jnp.log(summed)
    both(5, o_in.at[pl.ds(0, 7)]).wait_recv()
    result = jnp.zeros((PIECE, DH), jnp.float32)
    for s in range(NZ):
        column = jnp.sum(jnp.where(diagonal, share[s:s + 1, :], 0.0), axis=1, keepdims=True)
        result = result + column * o_in[s].astype(jnp.float32)
    result = result.astype(jnp.bfloat16)

    mine = rows(tg * 16, 16)
    oa_mine = oa.at[mine, cols(hg * 256, 256)]
    ob_mine = ob.at[:, cols(xy * 128, 128)]
    oa[mine, cols(hg * 256, 128)] = result[0:16]
    oa[mine, cols(hg * 256 + 128, 128)] = result[16:32]
    ob[:, cols(xy * 128, 128)] = result[32:48]
    for k in z_order:
        put(oa_mine, oa_mine, 7, at_z(z_of(k)))
    for k in xy_order:
        put(ob_mine, ob_mine, 8, xy_to(k)[1])
    for k in z_order:
        put(lg.at[xy, z], lg.at[xy, z], 9, at_z(z_of(k)))
    a_out = out_ref.at[:, cols(xy * 512, 512)]
    b_out = out_ref.at[mine, cols(A_COLS + hg * 1024, 1024)]
    both(7, s2a.at[pl.ds(0, 7)]).wait_recv()
    for k in xy_order:
        put(oa, a_out, 10, xy_to(k)[1])
    keep_a = pltpu.make_async_copy(oa, a_out, loc_sem.at[0])
    keep_a.start()
    both(8, s2b.at[pl.ds(0, 7)]).wait_recv()
    for k in z_order:
        put(ob, b_out, 11, at_z(z_of(k)))
    keep_b = pltpu.make_async_copy(ob, b_out, loc_sem.at[1])
    keep_b.start()
    both(9, st_in.at[pl.ds(0, 7)]).wait_recv()
    for k in xy_order:
        put(lg.at[xy], lg.at[xy], 12, xy_to(k)[1])

    both(12, lg.at[pl.ds(0, 7)]).wait_recv()
    t_group, t_in = me // 16, lax.rem(me, 16)
    lane = lax.broadcasted_iota(jnp.int32, (NXY, DH), 1)
    source = lax.broadcasted_iota(jnp.int32, (NXY, DH), 0)
    logs = jnp.zeros((NXY, DH), jnp.float32)
    for b in range(2):
        part = jnp.concatenate([lg[c, 2 * t_group + b] for c in range(NXY)], axis=0)
        for c in range(3):
            column = jnp.sum(jnp.where(lane == 16 * c + t_in, part, 0.0), axis=1, keepdims=True)
            head = source * 4 + 2 * b + c if c < 2 else 32 + 8 * b + source
            logs = logs + jnp.where(lane == head, column, 0.0)
    log_ref[...] = jnp.sum(logs, axis=0, keepdims=True)[:, :H]

    both(10, s1a.at[pl.ds(0, 7)]).wait_recv()
    both(11, s1b.at[pl.ds(0, 7)]).wait_recv()
    for stage, like in enumerate((s1a, s1b, s2a, s2b, qg, o_in, st_in, s2a, s2b, st_in, s1a, s1b, lg)):
        both(stage, like.at[pl.ds(0, 7)]).wait_send()
    for copy in kv_sent:
        copy.wait_send()
    keep_a.wait()
    keep_b.wait()


def body(queries, keys, values, query_host, lengths):
    bf16, f32 = jnp.bfloat16, jnp.float32
    attended, log_total = pl.pallas_call(
        kernel,
        out_shape=(
            jax.ShapeDtypeStruct((T, HD), bf16),
            jax.ShapeDtypeStruct((1, H), f32),
        ),
        in_specs=[
            pl.BlockSpec(memory_space=pl.ANY),
            pl.BlockSpec(memory_space=pl.ANY),
            pl.BlockSpec(memory_space=pl.ANY),
            pl.BlockSpec(memory_space=pl.ANY),
            pl.BlockSpec(memory_space=pl.ANY),
        ],
        out_specs=(
            pl.BlockSpec(memory_space=pl.ANY),
            pl.BlockSpec(memory_space=pltpu.VMEM),
        ),
        scratch_shapes=[
            pltpu.SMEM((1,), jnp.int32),
            pltpu.SMEM((1, 1), jnp.int32),
            pltpu.VMEM((NXY, 2 * KEYS + 16, DH), bf16),
            pltpu.VMEM((NXY, T, 512), bf16),
            pltpu.VMEM((NZ, 16, 1024), bf16),
            pltpu.VMEM((NZ, 16, 256), bf16),
            pltpu.VMEM((NXY, 16, 128), bf16),
            pltpu.VMEM((NZ, 16, 256), bf16),
            pltpu.VMEM((NXY, 16, 128), bf16),
            pltpu.VMEM((NZ, 16, 384), bf16),
            pltpu.VMEM((ROWS, DH), bf16),
            pltpu.VMEM((ROWS, 2 * DH), f32),
            pltpu.VMEM((ROWS, DH), f32),
            pltpu.VMEM((NZ, PIECE, DH), bf16),
            pltpu.VMEM((NZ, 1, DH), f32),
            pltpu.VMEM((NZ, PIECE, DH), bf16),
            pltpu.VMEM((NZ, 1, DH), f32),
            pltpu.VMEM((T, 512), bf16),
            pltpu.VMEM((16, 1024), bf16),
            pltpu.VMEM((NXY, NZ, 1, DH), f32),
            pltpu.SemaphoreType.DMA((6,)),
            pltpu.SemaphoreType.DMA((9,)),
            pltpu.SemaphoreType.DMA((9,)),
            pltpu.SemaphoreType.DMA((13,)),
            pltpu.SemaphoreType.DMA((13,)),
        ],
        compiler_params=pltpu.CompilerParams(
            collective_id=0, has_side_effects=True, vmem_limit_bytes=60 * 2**20),
    )(query_host, lengths, queries.reshape(T, HD), keys.reshape(KEYS, DH), values.reshape(KEYS, DH))
    return attended[None], log_total[None]


def solution(mesh):
    return jax.shard_map(
        body,
        mesh=mesh,
        in_specs=(
            P("req", "ctx", None, None),
            P("req", "ctx", None),
            P("req", "ctx", None),
            P("req"),
            P("req", "ctx"),
        ),
        out_specs=(P("req", None, None), P("req", "ctx", None)),
        check_vma=False,
    )
```

```python
import math

import jax
import jax.numpy as jnp
from jax import lax
from jax.experimental import pallas as pl
from jax.experimental.pallas import tpu as pltpu
from jax.sharding import PartitionSpec as P


H = 48
DH = 128
T = 64
KEYS = 512
BLOCK = 128
HD = H * DH
NZ = 8
NXY = 8
ROWS = 384
OWN = 16
PIECE = 48
A_COLS = 4096
NEG = -1e30
LOG2E = math.log2(math.e)
LN2 = math.log(2.0)
SCALE = DH ** -0.5 * LOG2E
MESH = pl.DeviceIdType.MESH


def kernel(host_in, len_in, q_ref, k_ref, v_ref, out_ref, log_ref,
           host_ref, len_ref, kv, s1a, s1b, x2a, x2b, s2a, s2b, qg, qm, acc, po, ps, o_in, st_in,
           oa, ob, lg, loc_sem, kv_send, kv_recv, send, recv):
    me = lax.axis_index("ctx")
    x, z, y = me // 32, (me // 4) % 8, me % 4
    xy = x * 4 + y
    tg, hg = z // 2, z % 2
    mine_kv, over_kv = x * 2 + y % 2, (1 - x) * 2 + y % 2

    def z_of(k):
        return lax.rem(z + k, NZ)

    def at_z(zz):
        return {"ctx": x * 32 + zz * 4 + y}

    def owner_to(k):
        zz = z_of(k % NZ)
        return zz + k // NZ * NZ, {"ctx": x * 32 + zz * 4 + (y if k < NZ else 3 - y)}

    def xy_to(k):
        px, py = lax.rem(x + k // 4, 2), lax.rem(y + k % 4, 4)
        return px * 4 + py, {"ctx": px * 32 + z * 4 + py}

    def put(src, dst, stage, device):
        pltpu.make_async_remote_copy(
            src_ref=src, dst_ref=dst, send_sem=send.at[stage], recv_sem=recv.at[stage],
            device_id=device, device_id_type=MESH).start()

    def both(stage, like):
        return pltpu.make_async_remote_copy(
            src_ref=like, dst_ref=like, send_sem=send.at[stage], recv_sem=recv.at[stage],
            device_id=at_z(z_of(1)), device_id_type=MESH)

    def cols(start, n):
        return pl.ds(pl.multiple_of(start, 128), n)

    def rows(start, n):
        return pl.ds(pl.multiple_of(start, 16), n)

    z_order = (4, 3, 5, 2, 6, 1, 7)
    xy_order = (6, 5, 7, 2, 4, 1, 3)
    owner_order = (12, 4, 11, 13, 3, 5, 10, 14, 2, 6, 9, 15, 1, 7, 8)

    def a_chunk(c):
        return q_ref.at[:, cols(c * 512, 512)]

    def b_chunk(zz):
        return q_ref.at[rows((zz // 2) * 16, 16), cols(A_COLS + lax.rem(zz, 2) * 1024, 1024)]

    barrier = pltpu.get_barrier_semaphore()
    for k in range(1, NZ):
        pl.semaphore_signal(barrier, inc=1, device_id=at_z(z_of(k)), device_id_type=MESH)
    for k in range(1, NXY):
        pl.semaphore_signal(barrier, inc=1, device_id=xy_to(k)[1], device_id_type=MESH)
    for k in range(9, 16):
        pl.semaphore_signal(barrier, inc=1, device_id=owner_to(k)[1], device_id_type=MESH)
    local = [
        pltpu.make_async_copy(len_in, len_ref, loc_sem.at[4]),
        pltpu.make_async_copy(host_in, host_ref, loc_sem.at[5]),
        pltpu.make_async_copy(k_ref, kv.at[mine_kv, pl.ds(0, KEYS)], loc_sem.at[0]),
        pltpu.make_async_copy(v_ref, kv.at[mine_kv, pl.ds(KEYS, KEYS)], loc_sem.at[1]),
        pltpu.make_async_copy(a_chunk(xy), s1a.at[xy], loc_sem.at[2]),
        pltpu.make_async_copy(b_chunk(z), s1b.at[z], loc_sem.at[3]),
    ]
    for copy in local:
        copy.start()
    local[0].wait()
    length = len_ref[0, 0].astype(jnp.float32)
    kv[mine_kv, 2 * KEYS:, :] = jnp.full((16, DH), length, jnp.float32).astype(jnp.bfloat16)
    local[1].wait()
    host = host_ref[0]
    host_z = lax.rem(host // 4, 8)
    host_xy = host // 32 * 4 + lax.rem(host, 4)
    pl.semaphore_wait(barrier, 21)

    for k in xy_order:
        c, device = xy_to(k)
        put(a_chunk(c), s1a.at[xy], 0, device)
    for k in z_order:
        zz = z_of(k)
        put(b_chunk(zz), s1b.at[z], 1, at_z(zz))
    local[2].wait()
    local[3].wait()
    over = {"ctx": (1 - x) * 32 + z * 4 + y}
    pair = {"ctx": x * 32 + z * 4 + y + 1 - y % 2 * 2}

    def kv_copy(slot, sem, device):
        return pltpu.make_async_remote_copy(
            src_ref=kv.at[slot], dst_ref=kv.at[slot], send_sem=kv_send.at[sem], recv_sem=kv_recv.at[sem],
            device_id=device, device_id_type=MESH)

    kv_sent = [kv_copy(mine_kv, 0, over), kv_copy(mine_kv, 1, pair), kv_copy(over_kv, 2, pair)]
    kv_got = [
        kv_copy(over_kv, 0, over),
        kv_copy(x * 2 + 1 - y % 2, 1, pair),
        kv_copy((1 - x) * 2 + 1 - y % 2, 2, pair),
    ]
    kv_sent[0].start()
    kv_sent[1].start()

    local[4].wait()
    both(0, s1a.at[pl.ds(0, 7)]).wait_recv()
    chunk = s1a[host_xy]
    for p in range(NZ):
        a, b = p // 2, p % 2
        x2a[p] = chunk[16 * a:16 * a + 16, 256 * b:256 * b + 256]
    s2a[z] = x2a[z]
    for k in z_order:
        zz = z_of(k)
        put(x2a.at[zz], s2a.at[z], 2, at_z(zz))
    local[5].wait()
    both(1, s1b.at[pl.ds(0, 7)]).wait_recv()
    chunk = s1b[host_z]
    for p in range(NXY):
        x2b[p] = chunk[:, 128 * p:128 * p + 128]
    s2b[xy] = x2b[xy]
    for k in xy_order:
        c, device = xy_to(k)
        put(x2b.at[c], s2b.at[xy], 3, device)

    kv_got[0].wait_recv()
    kv_sent[2].start()

    both(2, s2a.at[pl.ds(0, 7)]).wait_recv()
    both(3, s2b.at[pl.ds(0, 7)]).wait_recv()
    qg[z, :, 0:256] = s2a[host_z]
    qg[z, :, 256:384] = s2b[host_xy]
    for k in owner_order:
        n, device = owner_to(k)
        put(qg.at[z], qg.at[z + k // NZ * NZ], 4, device)
    kv_got[1].wait_recv()
    kv_got[2].wait_recv()

    block_id = (lax.broadcasted_iota(jnp.int32, (1, KEYS), 1) // BLOCK).astype(jnp.float32)
    lane = lax.broadcasted_iota(jnp.int32, (PIECE, DH), 1)
    diagonal = lane == lax.broadcasted_iota(jnp.int32, (PIECE, DH), 0)
    both(4, qg.at[pl.ds(0, OWN - 1)]).wait_recv()

    def attend(half):
        for p in range(NZ):
            for c in range(3):
                qm[half, PIECE * p + 16 * c:PIECE * p + 16 * c + 16, :] = (
                    qg[half * NZ + p, :, 128 * c:128 * c + 128])
        old = total = None
        for c in range(4):
            valid = kv[c, 2 * KEYS:2 * KEYS + 16, :].astype(jnp.float32)[0:1, :]
            valid = jnp.concatenate([valid] * (KEYS // DH), axis=1)
            score = lax.dot_general(
                qm[half], kv[c, 0:KEYS, :], (((1,), (1,)), ((), ())), preferred_element_type=jnp.float32)
            score = jnp.where(block_id < valid, score * SCALE, NEG)
            new = jnp.max(score, axis=1, keepdims=True)
            if c:
                new = jnp.maximum(old, new)
            weight = jnp.exp2(score - new).astype(jnp.bfloat16)
            value = jnp.concatenate(
                [kv[c, KEYS:2 * KEYS, :], jnp.ones((KEYS, DH), jnp.bfloat16)], axis=1)
            summed = jnp.dot(weight, value, preferred_element_type=jnp.float32)
            acc[half] = acc[half] * jnp.exp2(old - new) + summed if c else summed
            old = new
        total = acc[half, :, DH:]
        po[half * NZ:half * NZ + NZ] = (
            acc[half, :, :DH] / total).astype(jnp.bfloat16).reshape(NZ, PIECE, DH)
        lse = old + jnp.log(total) * LOG2E
        for p in range(NZ):
            part = lse[PIECE * p:PIECE * p + PIECE, :]
            ps[half * NZ + p] = jnp.sum(jnp.where(diagonal, part, 0.0), axis=0, keepdims=True)
        if half == 0:
            o_in[z] = po[z]
            st_in[z] = ps[z]
        for k in owner_order:
            if k // NZ == half:
                n, device = owner_to(k)
                put(po.at[n], o_in.at[half * NZ + z], 5, device)
                put(ps.at[n], st_in.at[half * NZ + z], 6, device)

    attend(1)
    attend(0)
    both(6, st_in.at[pl.ds(0, OWN - 1)]).wait_recv()
    stat = jnp.concatenate([st_in[s] for s in range(OWN)], axis=0)
    overall = jnp.max(stat, axis=0, keepdims=True)
    share = jnp.exp2(stat - overall)
    summed = jnp.sum(share, axis=0, keepdims=True)
    share = share / summed
    lg[xy, z] = overall * LN2 + jnp.log(summed)
    both(5, o_in.at[pl.ds(0, OWN - 1)]).wait_recv()
    result = jnp.zeros((PIECE, DH), jnp.float32)
    for s in range(OWN):
        column = jnp.sum(jnp.where(diagonal, share[s:s + 1, :], 0.0), axis=1, keepdims=True)
        result = result + column * o_in[s].astype(jnp.float32)
    result = result.astype(jnp.bfloat16)

    mine = rows(tg * 16, 16)
    oa_mine = oa.at[mine, cols(hg * 256, 256)]
    ob_mine = ob.at[:, cols(xy * 128, 128)]
    oa[mine, cols(hg * 256, 128)] = result[0:16]
    oa[mine, cols(hg * 256 + 128, 128)] = result[16:32]
    ob[:, cols(xy * 128, 128)] = result[32:48]
    for k in z_order:
        put(oa_mine, oa_mine, 7, at_z(z_of(k)))
    for k in xy_order:
        put(ob_mine, ob_mine, 8, xy_to(k)[1])
    for k in z_order:
        put(lg.at[xy, z], lg.at[xy, z], 9, at_z(z_of(k)))
    a_out = out_ref.at[:, cols(xy * 512, 512)]
    b_out = out_ref.at[mine, cols(A_COLS + hg * 1024, 1024)]
    both(7, s2a.at[pl.ds(0, 7)]).wait_recv()
    for k in xy_order:
        put(oa, a_out, 10, xy_to(k)[1])
    keep_a = pltpu.make_async_copy(oa, a_out, loc_sem.at[0])
    keep_a.start()
    both(8, s2b.at[pl.ds(0, 7)]).wait_recv()
    for k in z_order:
        put(ob, b_out, 11, at_z(z_of(k)))
    keep_b = pltpu.make_async_copy(ob, b_out, loc_sem.at[1])
    keep_b.start()
    both(9, ps.at[pl.ds(0, 7)]).wait_recv()
    for k in xy_order:
        put(lg.at[xy], lg.at[xy], 12, xy_to(k)[1])

    both(12, lg.at[pl.ds(0, 7)]).wait_recv()
    t_group, t_in = me // 16, lax.rem(me, 16)
    lane = lax.broadcasted_iota(jnp.int32, (NXY, DH), 1)
    source = lax.broadcasted_iota(jnp.int32, (NXY, DH), 0)
    logs = jnp.zeros((NXY, DH), jnp.float32)
    for b in range(2):
        part = jnp.concatenate([lg[c, 2 * t_group + b] for c in range(NXY)], axis=0)
        for c in range(3):
            column = jnp.sum(jnp.where(lane == 16 * c + t_in, part, 0.0), axis=1, keepdims=True)
            head = source * 4 + 2 * b + c if c < 2 else 32 + 8 * b + source
            logs = logs + jnp.where(lane == head, column, 0.0)
    log_ref[...] = jnp.sum(logs, axis=0, keepdims=True)[:, :H]

    both(10, s1a.at[pl.ds(0, 7)]).wait_recv()
    both(11, s1b.at[pl.ds(0, 7)]).wait_recv()
    for stage, like in enumerate((s1a, s1b, s2a, s2b, None, None, None, s2a, s2b, ps, s1a, s1b, lg)):
        if like is not None:
            both(stage, like.at[pl.ds(0, 7)]).wait_send()
    for stage, like in ((4, qg), (5, o_in), (6, st_in)):
        both(stage, like.at[pl.ds(0, OWN - 1)]).wait_send()
    for copy in kv_sent:
        copy.wait_send()
    keep_a.wait()
    keep_b.wait()


def body(queries, keys, values, query_host, lengths):
    bf16, f32 = jnp.bfloat16, jnp.float32
    attended, log_total = pl.pallas_call(
        kernel,
        out_shape=(
            jax.ShapeDtypeStruct((T, HD), bf16),
            jax.ShapeDtypeStruct((1, H), f32),
        ),
        in_specs=[
            pl.BlockSpec(memory_space=pl.ANY),
            pl.BlockSpec(memory_space=pl.ANY),
            pl.BlockSpec(memory_space=pl.ANY),
            pl.BlockSpec(memory_space=pl.ANY),
            pl.BlockSpec(memory_space=pl.ANY),
        ],
        out_specs=(
            pl.BlockSpec(memory_space=pl.ANY),
            pl.BlockSpec(memory_space=pltpu.VMEM),
        ),
        scratch_shapes=[
            pltpu.SMEM((1,), jnp.int32),
            pltpu.SMEM((1, 1), jnp.int32),
            pltpu.VMEM((4, 2 * KEYS + 16, DH), bf16),
            pltpu.VMEM((NXY, T, 512), bf16),
            pltpu.VMEM((NZ, 16, 1024), bf16),
            pltpu.VMEM((NZ, 16, 256), bf16),
            pltpu.VMEM((NXY, 16, 128), bf16),
            pltpu.VMEM((NZ, 16, 256), bf16),
            pltpu.VMEM((NXY, 16, 128), bf16),
            pltpu.VMEM((OWN, 16, 384), bf16),
            pltpu.VMEM((2, ROWS, DH), bf16),
            pltpu.VMEM((2, ROWS, 2 * DH), f32),
            pltpu.VMEM((OWN, PIECE, DH), bf16),
            pltpu.VMEM((OWN, 1, DH), f32),
            pltpu.VMEM((OWN, PIECE, DH), bf16),
            pltpu.VMEM((OWN, 1, DH), f32),
            pltpu.VMEM((T, 512), bf16),
            pltpu.VMEM((16, 1024), bf16),
            pltpu.VMEM((NXY, NZ, 1, DH), f32),
            pltpu.SemaphoreType.DMA((6,)),
            pltpu.SemaphoreType.DMA((3,)),
            pltpu.SemaphoreType.DMA((3,)),
            pltpu.SemaphoreType.DMA((13,)),
            pltpu.SemaphoreType.DMA((13,)),
        ],
        compiler_params=pltpu.CompilerParams(
            collective_id=0, has_side_effects=True, vmem_limit_bytes=60 * 2**20),
    )(query_host, lengths, queries.reshape(T, HD), keys.reshape(KEYS, DH), values.reshape(KEYS, DH))
    return attended[None], log_total[None]


def solution(mesh):
    return jax.shard_map(
        body,
        mesh=mesh,
        in_specs=(
            P("req", "ctx", None, None),
            P("req", "ctx", None),
            P("req", "ctx", None),
            P("req"),
            P("req", "ctx"),
        ),
        out_specs=(P("req", None, None), P("req", "ctx", None)),
        check_vma=False,
    )
```

```python
import math

import jax
import jax.numpy as jnp
from jax import lax
from jax.experimental import pallas as pl
from jax.experimental.pallas import tpu as pltpu
from jax.sharding import PartitionSpec as P


H = 48
DH = 128
T = 64
KEYS = 512
BLOCK = 128
HD = H * DH
NZ = 8
NXY = 8
ROWS = 384
OWN = 16
PIECE = 48
A_COLS = 4096
NEG = -1e30
LOG2E = math.log2(math.e)
LN2 = math.log(2.0)
SCALE = DH ** -0.5 * LOG2E
MESH = pl.DeviceIdType.MESH


def kernel(host_in, len_in, q_ref, k_ref, v_ref, out_ref, log_out,
           host_ref, len_ref, kv, s1a, s1b, x2a, x2b, s2a, s2b, qg, qm, acc, po, ps, o_in, st_in,
           oa, ob, lg, log_ref, loc_sem, kv_send, kv_recv, send, recv):
    me = lax.axis_index("ctx")
    x, z, y = me // 32, (me // 4) % 8, me % 4
    xy = x * 4 + y
    tg, hg = z // 2, z % 2
    mine_kv, over_kv = x * 2 + y % 2, (1 - x) * 2 + y % 2

    def z_of(k):
        return lax.rem(z + k, NZ)

    def at_z(zz):
        return {"ctx": x * 32 + zz * 4 + y}

    def owner_to(k):
        zz = z_of(k % NZ)
        return zz + k // NZ * NZ, {"ctx": x * 32 + zz * 4 + (y if k < NZ else 3 - y)}

    def xy_to(k):
        px, py = lax.rem(x + k // 4, 2), lax.rem(y + k % 4, 4)
        return px * 4 + py, {"ctx": px * 32 + z * 4 + py}

    def put(src, dst, stage, device):
        pltpu.make_async_remote_copy(
            src_ref=src, dst_ref=dst, send_sem=send.at[stage], recv_sem=recv.at[stage],
            device_id=device, device_id_type=MESH).start()

    def both(stage, like):
        return pltpu.make_async_remote_copy(
            src_ref=like, dst_ref=like, send_sem=send.at[stage], recv_sem=recv.at[stage],
            device_id=at_z(z_of(1)), device_id_type=MESH)

    def cols(start, n):
        return pl.ds(pl.multiple_of(start, 128), n)

    def rows(start, n):
        return pl.ds(pl.multiple_of(start, 16), n)

    z_order = (4, 3, 5, 2, 6, 1, 7)
    xy_order = (6, 5, 7, 2, 4, 1, 3)
    owner_order = (12, 4, 11, 13, 3, 5, 10, 14, 2, 6, 9, 15, 1, 7, 8)

    def a_chunk(c):
        return q_ref.at[:, cols(c * 512, 512)]

    def b_chunk(zz):
        return q_ref.at[rows((zz // 2) * 16, 16), cols(A_COLS + lax.rem(zz, 2) * 1024, 1024)]

    barrier = pltpu.get_barrier_semaphore()
    for k in (4, 3, 5):
        pl.semaphore_signal(barrier, inc=1, device_id=at_z(z_of(k)), device_id_type=MESH)
    for k in (6, 5, 7):
        pl.semaphore_signal(barrier, inc=1, device_id=xy_to(k)[1], device_id_type=MESH)
    for k in ():
        pl.semaphore_signal(barrier, inc=1, device_id=owner_to(k)[1], device_id_type=MESH)
    for k in (2, 6):
        pl.semaphore_signal(barrier, inc=1, device_id=at_z(z_of(k)), device_id_type=MESH)
    for k in (2, 4, 1, 3):
        pl.semaphore_signal(barrier, inc=1, device_id=xy_to(k)[1], device_id_type=MESH)
    for k in ():
        pl.semaphore_signal(barrier, inc=1, device_id=owner_to(k)[1], device_id_type=MESH)
    for k in (1, 7):
        pl.semaphore_signal(barrier, inc=1, device_id=at_z(z_of(k)), device_id_type=MESH)
    for k in ():
        pl.semaphore_signal(barrier, inc=1, device_id=xy_to(k)[1], device_id_type=MESH)
    for k in ():
        pl.semaphore_signal(barrier, inc=1, device_id=owner_to(k)[1], device_id_type=MESH)
    local = [
        pltpu.make_async_copy(len_in, len_ref, loc_sem.at[4]),
        pltpu.make_async_copy(host_in, host_ref, loc_sem.at[5]),
        pltpu.make_async_copy(k_ref, kv.at[mine_kv, pl.ds(0, KEYS)], loc_sem.at[0]),
        pltpu.make_async_copy(v_ref, kv.at[mine_kv, pl.ds(KEYS, KEYS)], loc_sem.at[1]),
        pltpu.make_async_copy(a_chunk(xy), s1a.at[xy], loc_sem.at[2]),
        pltpu.make_async_copy(b_chunk(z), s1b.at[z], loc_sem.at[3]),
    ]
    for copy in local:
        copy.start()
    pl.semaphore_wait(barrier, 14)

    for k in xy_order:
        c, device = xy_to(k)
        put(a_chunk(c), s1a.at[xy], 0, device)
    for k in z_order:
        zz = z_of(k)
        put(b_chunk(zz), s1b.at[z], 1, at_z(zz))
    local[0].wait()
    length = len_ref[0, 0].astype(jnp.float32)
    kv[mine_kv, 2 * KEYS:, :] = jnp.full((16, DH), length, jnp.float32).astype(jnp.bfloat16)
    local[2].wait()
    local[3].wait()
    over = {"ctx": (1 - x) * 32 + z * 4 + y}
    pair = {"ctx": x * 32 + z * 4 + y + 1 - y % 2 * 2}

    def kv_copy(slot, sem, device):
        return pltpu.make_async_remote_copy(
            src_ref=kv.at[slot], dst_ref=kv.at[slot], send_sem=kv_send.at[sem], recv_sem=kv_recv.at[sem],
            device_id=device, device_id_type=MESH)

    kv_sent = [kv_copy(mine_kv, 0, over), kv_copy(mine_kv, 1, pair), kv_copy(over_kv, 2, pair)]
    kv_got = [
        kv_copy(over_kv, 0, over),
        kv_copy(x * 2 + 1 - y % 2, 1, pair),
        kv_copy((1 - x) * 2 + 1 - y % 2, 2, pair),
    ]
    kv_sent[0].start()
    kv_sent[1].start()

    local[1].wait()
    host = host_ref[0]
    host_z = lax.rem(host // 4, 8)
    host_xy = host // 32 * 4 + lax.rem(host, 4)
    local[4].wait()
    both(0, s1a.at[pl.ds(0, 7)]).wait_recv()
    chunk = s1a[host_xy]
    for p in range(NZ):
        a, b = p // 2, p % 2
        x2a[p] = chunk[16 * a:16 * a + 16, 256 * b:256 * b + 256]
    s2a[z] = x2a[z]
    for k in z_order:
        zz = z_of(k)
        put(x2a.at[zz], s2a.at[z], 2, at_z(zz))
    local[5].wait()
    both(1, s1b.at[pl.ds(0, 7)]).wait_recv()
    chunk = s1b[host_z]
    for p in range(NXY):
        x2b[p] = chunk[:, 128 * p:128 * p + 128]
    s2b[xy] = x2b[xy]
    for k in xy_order:
        c, device = xy_to(k)
        put(x2b.at[c], s2b.at[xy], 3, device)

    kv_got[0].wait_recv()
    kv_sent[2].start()

    both(2, s2a.at[pl.ds(0, 7)]).wait_recv()
    both(3, s2b.at[pl.ds(0, 7)]).wait_recv()
    qg[z, :, 0:256] = s2a[host_z]
    qg[z, :, 256:384] = s2b[host_xy]
    for k in owner_order:
        n, device = owner_to(k)
        put(qg.at[z], qg.at[z + k // NZ * NZ], 4, device)
    kv_got[1].wait_recv()
    kv_got[2].wait_recv()

    block_id = (lax.broadcasted_iota(jnp.int32, (1, KEYS), 1) // BLOCK).astype(jnp.float32)
    lane = lax.broadcasted_iota(jnp.int32, (PIECE, DH), 1)
    diagonal = lane == lax.broadcasted_iota(jnp.int32, (PIECE, DH), 0)
    both(4, qg.at[pl.ds(0, OWN - 1)]).wait_recv()

    def attend(group, ks):
        targets = [owner_to(k) for k in ks]
        size = PIECE * len(ks)
        for i, (n, _) in enumerate(targets):
            for c in range(3):
                qm[group, PIECE * i + 16 * c:PIECE * i + 16 * c + 16, :] = qg[n, :, 128 * c:128 * c + 128]
        old = total = None
        for c in range(4):
            valid = kv[c, 2 * KEYS:2 * KEYS + 16, :].astype(jnp.float32)[0:1, :]
            valid = jnp.concatenate([valid] * (KEYS // DH), axis=1)
            score = lax.dot_general(
                qm[group, 0:size, :], kv[c, 0:KEYS, :], (((1,), (1,)), ((), ())),
                preferred_element_type=jnp.float32)
            score = jnp.where(block_id < valid, score * SCALE, NEG)
            new = jnp.max(score, axis=1, keepdims=True)
            if c:
                new = jnp.maximum(old, new)
            weight = jnp.exp2(score - new).astype(jnp.bfloat16)
            value = jnp.concatenate(
                [kv[c, KEYS:2 * KEYS, :], jnp.ones((KEYS, DH), jnp.bfloat16)], axis=1)
            summed = jnp.dot(weight, value, preferred_element_type=jnp.float32)
            acc[group, 0:size, :] = acc[group, 0:size, :] * jnp.exp2(old - new) + summed if c else summed
            old = new
        total = acc[group, 0:size, DH:]
        part = (acc[group, 0:size, :DH] / total).astype(jnp.bfloat16)
        lse = old + jnp.log(total) * LOG2E
        for i, (k, (n, device)) in enumerate(zip(ks, targets)):
            at = slice(PIECE * i, PIECE * i + PIECE)
            stat = jnp.sum(jnp.where(diagonal, lse[at, :], 0.0), axis=0, keepdims=True)
            if k:
                po[n], ps[n] = part[at, :], stat
                put(po.at[n], o_in.at[k // NZ * NZ + z], 5, device)
                put(ps.at[n], st_in.at[k // NZ * NZ + z], 6, device)
            else:
                o_in[z], st_in[z] = part[at, :], stat

    for group, ks in enumerate(((12, 11, 13, 4), (10, 14, 3, 5), (9, 15, 2, 6), (8, 1, 7, 0))):
        attend(group, ks)
    both(6, st_in.at[pl.ds(0, OWN - 1)]).wait_recv()
    stat = jnp.concatenate([st_in[s] for s in range(OWN)], axis=0)
    overall = jnp.max(stat, axis=0, keepdims=True)
    share = jnp.exp2(stat - overall)
    summed = jnp.sum(share, axis=0, keepdims=True)
    share = share / summed
    lg[xy, z] = overall * LN2 + jnp.log(summed)
    for k in z_order:
        put(lg.at[xy, z], lg.at[xy, z], 9, at_z(z_of(k)))
    both(5, o_in.at[pl.ds(0, OWN - 1)]).wait_recv()
    result = jnp.zeros((PIECE, DH), jnp.float32)
    for s in range(OWN):
        column = jnp.sum(jnp.where(diagonal, share[s:s + 1, :], 0.0), axis=1, keepdims=True)
        result = result + column * o_in[s].astype(jnp.float32)
    result = result.astype(jnp.bfloat16)

    mine = rows(tg * 16, 16)
    oa_mine = oa.at[mine, cols(hg * 256, 256)]
    ob_mine = ob.at[:, cols(xy * 128, 128)]
    oa[mine, cols(hg * 256, 128)] = result[0:16]
    oa[mine, cols(hg * 256 + 128, 128)] = result[16:32]
    ob[:, cols(xy * 128, 128)] = result[32:48]
    for k in z_order:
        put(oa_mine, oa_mine, 7, at_z(z_of(k)))
    for k in xy_order:
        put(ob_mine, ob_mine, 8, xy_to(k)[1])
    both(9, ps.at[pl.ds(0, 7)]).wait_recv()
    for k in xy_order:
        put(lg.at[xy], lg.at[xy], 12, xy_to(k)[1])
    a_out = out_ref.at[:, cols(xy * 512, 512)]
    b_out = out_ref.at[mine, cols(A_COLS + hg * 1024, 1024)]
    both(7, s2a.at[pl.ds(0, 7)]).wait_recv()
    for k in xy_order:
        put(oa, a_out, 10, xy_to(k)[1])
    keep_a = pltpu.make_async_copy(oa, a_out, loc_sem.at[0])
    keep_a.start()
    both(8, s2b.at[pl.ds(0, 7)]).wait_recv()
    for k in z_order:
        put(ob, b_out, 11, at_z(z_of(k)))
    keep_b = pltpu.make_async_copy(ob, b_out, loc_sem.at[1])
    keep_b.start()

    both(12, lg.at[pl.ds(0, 7)]).wait_recv()
    t_group, t_in = me // 16, lax.rem(me, 16)
    lane = lax.broadcasted_iota(jnp.int32, (NXY, DH), 1)
    source = lax.broadcasted_iota(jnp.int32, (NXY, DH), 0)
    logs = jnp.zeros((NXY, DH), jnp.float32)
    for b in range(2):
        part = jnp.concatenate([lg[c, 2 * t_group + b] for c in range(NXY)], axis=0)
        for c in range(3):
            column = jnp.sum(jnp.where(lane == 16 * c + t_in, part, 0.0), axis=1, keepdims=True)
            head = source * 4 + 2 * b + c if c < 2 else 32 + 8 * b + source
            logs = logs + jnp.where(lane == head, column, 0.0)
    log_ref[...] = jnp.sum(logs, axis=0, keepdims=True)[:, :H]
    keep_log = pltpu.make_async_copy(log_ref, log_out, loc_sem.at[2])
    keep_log.start()

    both(10, s1a.at[pl.ds(0, 7)]).wait_recv()
    both(11, s1b.at[pl.ds(0, 7)]).wait_recv()
    for stage, like in enumerate((s1a, s1b, s2a, s2b, None, None, None, s2a, s2b, ps, s1a, s1b, lg)):
        if like is not None:
            both(stage, like.at[pl.ds(0, 7)]).wait_send()
    for stage, like in ((4, qg), (5, o_in), (6, st_in)):
        both(stage, like.at[pl.ds(0, OWN - 1)]).wait_send()
    for copy in kv_sent:
        copy.wait_send()
    keep_a.wait()
    keep_b.wait()
    keep_log.wait()


def body(queries, keys, values, query_host, lengths):
    bf16, f32 = jnp.bfloat16, jnp.float32
    attended, log_total = pl.pallas_call(
        kernel,
        out_shape=(
            jax.ShapeDtypeStruct((T, HD), bf16),
            jax.ShapeDtypeStruct((1, H), f32),
        ),
        in_specs=[
            pl.BlockSpec(memory_space=pl.ANY),
            pl.BlockSpec(memory_space=pl.ANY),
            pl.BlockSpec(memory_space=pl.ANY),
            pl.BlockSpec(memory_space=pl.ANY),
            pl.BlockSpec(memory_space=pl.ANY),
        ],
        out_specs=(
            pl.BlockSpec(memory_space=pl.ANY),
            pl.BlockSpec(memory_space=pl.ANY),
        ),
        scratch_shapes=[
            pltpu.SMEM((1,), jnp.int32),
            pltpu.SMEM((1, 1), jnp.int32),
            pltpu.VMEM((4, 2 * KEYS + 16, DH), bf16),
            pltpu.VMEM((NXY, T, 512), bf16),
            pltpu.VMEM((NZ, 16, 1024), bf16),
            pltpu.VMEM((NZ, 16, 256), bf16),
            pltpu.VMEM((NXY, 16, 128), bf16),
            pltpu.VMEM((NZ, 16, 256), bf16),
            pltpu.VMEM((NXY, 16, 128), bf16),
            pltpu.VMEM((OWN, 16, 384), bf16),
            pltpu.VMEM((4, ROWS, DH), bf16),
            pltpu.VMEM((4, ROWS, 2 * DH), f32),
            pltpu.VMEM((OWN, PIECE, DH), bf16),
            pltpu.VMEM((OWN, 1, DH), f32),
            pltpu.VMEM((OWN, PIECE, DH), bf16),
            pltpu.VMEM((OWN, 1, DH), f32),
            pltpu.VMEM((T, 512), bf16),
            pltpu.VMEM((16, 1024), bf16),
            pltpu.VMEM((NXY, NZ, 1, DH), f32),
            pltpu.VMEM((1, H), f32),
            pltpu.SemaphoreType.DMA((6,)),
            pltpu.SemaphoreType.DMA((3,)),
            pltpu.SemaphoreType.DMA((3,)),
            pltpu.SemaphoreType.DMA((13,)),
            pltpu.SemaphoreType.DMA((13,)),
        ],
        compiler_params=pltpu.CompilerParams(
            collective_id=0, has_side_effects=True, vmem_limit_bytes=60 * 2**20),
    )(query_host, lengths, queries.reshape(T, HD), keys.reshape(KEYS, DH), values.reshape(KEYS, DH))
    return attended[None], log_total[None]


def solution(mesh):
    return jax.shard_map(
        body,
        mesh=mesh,
        in_specs=(
            P("req", "ctx", None, None),
            P("req", "ctx", None),
            P("req", "ctx", None),
            P("req"),
            P("req", "ctx"),
        ),
        out_specs=(P("req", None, None), P("req", "ctx", None)),
        check_vma=False,
    )
```

```python
import math

import jax
import jax.numpy as jnp
from jax import lax
from jax.experimental import pallas as pl
from jax.experimental.pallas import tpu as pltpu
from jax.sharding import PartitionSpec as P


H = 48
DH = 128
T = 64
KEYS = 512
BLOCK = 128
HD = H * DH
NZ = 8
NXY = 8
ROWS = 384
OWN = 16
PIECE = 48
A_COLS = 4096
NEG = -1e30
LOG2E = math.log2(math.e)
LN2 = math.log(2.0)
SCALE = DH ** -0.5 * LOG2E
MESH = pl.DeviceIdType.MESH


def kernel(host_in, len_in, q_ref, k_ref, v_ref, out_ref, log_out,
           host_ref, len_ref, kv, s1a, s1b, x2a, x2b, s2a, s2b, qg, qm, acc, po, ps, o_in, st_in,
           oa, ob, lg, log_ref, loc_sem, kv_send, kv_recv, send, recv):
    me = lax.axis_index("ctx")
    x, z, y = me // 32, (me // 4) % 8, me % 4
    xy = x * 4 + y
    tg, hg = z // 2, z % 2
    mine_kv, over_kv = x * 2 + y % 2, (1 - x) * 2 + y % 2

    def z_of(k):
        return lax.rem(z + k, NZ)

    def at_z(zz):
        return {"ctx": x * 32 + zz * 4 + y}

    def owner_to(k):
        zz = z_of(k % NZ)
        return zz + k // NZ * NZ, {"ctx": x * 32 + zz * 4 + (y if k < NZ else 3 - y)}

    def xy_to(k):
        px, py = lax.rem(x + k // 4, 2), lax.rem(y + k % 4, 4)
        return px * 4 + py, {"ctx": px * 32 + z * 4 + py}

    def put(src, dst, stage, device):
        pltpu.make_async_remote_copy(
            src_ref=src, dst_ref=dst, send_sem=send.at[stage], recv_sem=recv.at[stage],
            device_id=device, device_id_type=MESH).start()

    def both(stage, like):
        return pltpu.make_async_remote_copy(
            src_ref=like, dst_ref=like, send_sem=send.at[stage], recv_sem=recv.at[stage],
            device_id=at_z(z_of(1)), device_id_type=MESH)

    def cols(start, n):
        return pl.ds(pl.multiple_of(start, 128), n)

    def rows(start, n):
        return pl.ds(pl.multiple_of(start, 16), n)

    z_order = (4, 3, 5, 2, 6, 1, 7)
    xy_order = (6, 5, 7, 2, 4, 1, 3)
    owner_order = (12, 4, 11, 13, 3, 5, 10, 14, 2, 6, 9, 15, 1, 7, 8)

    def a_chunk(c):
        return q_ref.at[:, cols(c * 512, 512)]

    def b_chunk(zz):
        return q_ref.at[rows((zz // 2) * 16, 16), cols(A_COLS + lax.rem(zz, 2) * 1024, 1024)]

    barrier = pltpu.get_barrier_semaphore()
    for k in (4, 3, 5):
        pl.semaphore_signal(barrier, inc=1, device_id=at_z(z_of(k)), device_id_type=MESH)
    for k in (6, 5, 7):
        pl.semaphore_signal(barrier, inc=1, device_id=xy_to(k)[1], device_id_type=MESH)
    for k in ():
        pl.semaphore_signal(barrier, inc=1, device_id=owner_to(k)[1], device_id_type=MESH)
    for k in (2, 6):
        pl.semaphore_signal(barrier, inc=1, device_id=at_z(z_of(k)), device_id_type=MESH)
    for k in (2, 4, 1, 3):
        pl.semaphore_signal(barrier, inc=1, device_id=xy_to(k)[1], device_id_type=MESH)
    for k in ():
        pl.semaphore_signal(barrier, inc=1, device_id=owner_to(k)[1], device_id_type=MESH)
    for k in (1, 7):
        pl.semaphore_signal(barrier, inc=1, device_id=at_z(z_of(k)), device_id_type=MESH)
    for k in ():
        pl.semaphore_signal(barrier, inc=1, device_id=xy_to(k)[1], device_id_type=MESH)
    for k in ():
        pl.semaphore_signal(barrier, inc=1, device_id=owner_to(k)[1], device_id_type=MESH)
    local = [
        pltpu.make_async_copy(len_in, len_ref, loc_sem.at[4]),
        pltpu.make_async_copy(host_in, host_ref, loc_sem.at[5]),
        pltpu.make_async_copy(k_ref, kv.at[mine_kv, pl.ds(0, KEYS)], loc_sem.at[0]),
        pltpu.make_async_copy(v_ref, kv.at[mine_kv, pl.ds(KEYS, KEYS)], loc_sem.at[1]),
        pltpu.make_async_copy(a_chunk(xy), s1a.at[xy], loc_sem.at[2]),
        pltpu.make_async_copy(b_chunk(z), s1b.at[z], loc_sem.at[3]),
    ]
    for copy in local:
        copy.start()
    pl.semaphore_wait(barrier, 14)

    for k in xy_order:
        c, device = xy_to(k)
        put(a_chunk(c), s1a.at[xy], 0, device)
    for k in z_order:
        zz = z_of(k)
        put(b_chunk(zz), s1b.at[z], 1, at_z(zz))
    local[0].wait()
    length = len_ref[0, 0].astype(jnp.float32)
    kv[mine_kv, 2 * KEYS:, :] = jnp.full((16, DH), length, jnp.float32).astype(jnp.bfloat16)
    local[2].wait()
    local[3].wait()
    over = {"ctx": (1 - x) * 32 + z * 4 + y}
    pair = {"ctx": x * 32 + z * 4 + y + 1 - y % 2 * 2}

    def kv_copy(slot, sem, device):
        return pltpu.make_async_remote_copy(
            src_ref=kv.at[slot], dst_ref=kv.at[slot], send_sem=kv_send.at[sem], recv_sem=kv_recv.at[sem],
            device_id=device, device_id_type=MESH)

    kv_sent = [kv_copy(mine_kv, 0, over), kv_copy(mine_kv, 1, pair), kv_copy(over_kv, 2, pair)]
    kv_got = [
        kv_copy(over_kv, 0, over),
        kv_copy(x * 2 + 1 - y % 2, 1, pair),
        kv_copy((1 - x) * 2 + 1 - y % 2, 2, pair),
    ]
    kv_sent[0].start()
    kv_sent[1].start()

    local[1].wait()
    host = host_ref[0]
    host_z = lax.rem(host // 4, 8)
    host_xy = host // 32 * 4 + lax.rem(host, 4)
    local[4].wait()
    both(0, s1a.at[pl.ds(0, 7)]).wait_recv()
    chunk = s1a[host_xy]
    for p in range(NZ):
        a, b = p // 2, p % 2
        x2a[p] = chunk[16 * a:16 * a + 16, 256 * b:256 * b + 256]
    s2a[z] = x2a[z]
    for k in z_order:
        zz = z_of(k)
        put(x2a.at[zz], s2a.at[z], 2, at_z(zz))
    local[5].wait()
    both(1, s1b.at[pl.ds(0, 7)]).wait_recv()
    chunk = s1b[host_z]
    for p in range(NXY):
        x2b[p] = chunk[:, 128 * p:128 * p + 128]
    s2b[xy] = x2b[xy]
    for k in xy_order:
        c, device = xy_to(k)
        put(x2b.at[c], s2b.at[xy], 3, device)

    kv_got[0].wait_recv()
    kv_sent[2].start()

    both(2, s2a.at[pl.ds(0, 7)]).wait_recv()
    both(3, s2b.at[pl.ds(0, 7)]).wait_recv()
    qg[z, :, 0:256] = s2a[host_z]
    qg[z, :, 256:384] = s2b[host_xy]
    for k in owner_order:
        n, device = owner_to(k)
        put(qg.at[z], qg.at[z + k // NZ * NZ], 4, device)
    kv_got[1].wait_recv()
    kv_got[2].wait_recv()

    block_id = (lax.broadcasted_iota(jnp.int32, (1, KEYS), 1) // BLOCK).astype(jnp.float32)
    lane = lax.broadcasted_iota(jnp.int32, (PIECE, DH), 1)
    diagonal = lane == lax.broadcasted_iota(jnp.int32, (PIECE, DH), 0)
    both(4, qg.at[pl.ds(0, OWN - 1)]).wait_recv()

    def attend(group, ks):
        targets = [owner_to(k) for k in ks]
        size = PIECE * len(ks)
        for i, (n, _) in enumerate(targets):
            for c in range(3):
                qm[group, PIECE * i + 16 * c:PIECE * i + 16 * c + 16, :] = qg[n, :, 128 * c:128 * c + 128]
        old = total = None
        for c in range(4):
            valid = kv[c, 2 * KEYS:2 * KEYS + 16, :].astype(jnp.float32)[0:1, :]
            valid = jnp.concatenate([valid] * (KEYS // DH), axis=1)
            score = lax.dot_general(
                qm[group, 0:size, :], kv[c, 0:KEYS, :], (((1,), (1,)), ((), ())),
                preferred_element_type=jnp.float32)
            score = jnp.where(block_id < valid, score * SCALE, NEG)
            new = jnp.max(score, axis=1, keepdims=True)
            if c:
                new = jnp.maximum(old, new)
            weight = jnp.exp2(score - new).astype(jnp.bfloat16)
            value = jnp.concatenate(
                [kv[c, KEYS:2 * KEYS, :], jnp.ones((KEYS, DH), jnp.bfloat16)], axis=1)
            summed = jnp.dot(weight, value, preferred_element_type=jnp.float32)
            acc[group, 0:size, :] = acc[group, 0:size, :] * jnp.exp2(old - new) + summed if c else summed
            old = new
        total = acc[group, 0:size, DH:]
        part = (acc[group, 0:size, :DH] / total).astype(jnp.bfloat16)
        lse = old + jnp.log(total) * LOG2E
        for i, (k, (n, device)) in enumerate(zip(ks, targets)):
            at = slice(PIECE * i, PIECE * i + PIECE)
            stat = jnp.sum(jnp.where(diagonal, lse[at, :], 0.0), axis=0, keepdims=True)
            if k:
                po[n], ps[n] = part[at, :], stat
                put(po.at[n], o_in.at[k // NZ * NZ + z], 5, device)
                put(ps.at[n], st_in.at[k // NZ * NZ + z], 6, device)
            else:
                o_in[z], st_in[z] = part[at, :], stat

    for group, ks in enumerate(((12, 11, 13, 4), (10, 14, 3, 5), (9, 15, 2, 6), (8, 1, 7, 0))):
        attend(group, ks)
    both(6, st_in.at[pl.ds(0, OWN - 1)]).wait_recv()
    stat = jnp.concatenate([st_in[s] for s in range(OWN)], axis=0)
    overall = jnp.max(stat, axis=0, keepdims=True)
    share = jnp.exp2(stat - overall)
    summed = jnp.sum(share, axis=0, keepdims=True)
    share = share / summed
    lg[xy, z] = overall * LN2 + jnp.log(summed)
    for k in z_order:
        put(lg.at[xy, z], lg.at[xy, z], 9, at_z(z_of(k)))
    both(5, o_in.at[pl.ds(0, OWN - 1)]).wait_recv()
    result = jnp.zeros((PIECE, DH), jnp.float32)
    for s in range(OWN):
        column = jnp.sum(jnp.where(diagonal, share[s:s + 1, :], 0.0), axis=1, keepdims=True)
        result = result + column * o_in[s].astype(jnp.float32)
    result = result.astype(jnp.bfloat16)

    mine = rows(tg * 16, 16)
    oa_mine = oa.at[mine, cols(hg * 256, 256)]
    ob_mine = ob.at[:, cols(xy * 128, 128)]
    oa[mine, cols(hg * 256, 128)] = result[0:16]
    oa[mine, cols(hg * 256 + 128, 128)] = result[16:32]
    ob[:, cols(xy * 128, 128)] = result[32:48]
    for k in z_order:
        put(oa_mine, oa_mine, 7, at_z(z_of(k)))
    for k in xy_order:
        put(ob_mine, ob_mine, 8, xy_to(k)[1])
    both(9, ps.at[pl.ds(0, 7)]).wait_recv()
    for k in xy_order:
        put(lg.at[xy], lg.at[xy], 12, xy_to(k)[1])
    a_out = out_ref.at[:, cols(xy * 512, 512)]
    b_out = out_ref.at[mine, cols(A_COLS + hg * 1024, 1024)]
    both(7, s2a.at[pl.ds(0, 7)]).wait_recv()
    for k in xy_order:
        put(oa, a_out, 10, xy_to(k)[1])
    keep_a = pltpu.make_async_copy(oa, a_out, loc_sem.at[0])
    keep_a.start()
    both(8, s2b.at[pl.ds(0, 7)]).wait_recv()
    for k in z_order:
        put(ob, b_out, 11, at_z(z_of(k)))
    keep_b = pltpu.make_async_copy(ob, b_out, loc_sem.at[1])
    keep_b.start()

    both(12, lg.at[pl.ds(0, 7)]).wait_recv()
    t_group, t_in = me // 16, lax.rem(me, 16)
    lane = lax.broadcasted_iota(jnp.int32, (NXY, DH), 1)
    source = lax.broadcasted_iota(jnp.int32, (NXY, DH), 0)
    logs = jnp.zeros((NXY, DH), jnp.float32)
    for b in range(2):
        part = jnp.concatenate([lg[c, 2 * t_group + b] for c in range(NXY)], axis=0)
        for c in range(3):
            column = jnp.sum(jnp.where(lane == 16 * c + t_in, part, 0.0), axis=1, keepdims=True)
            head = source * 4 + 2 * b + c if c < 2 else 32 + 8 * b + source
            logs = logs + jnp.where(lane == head, column, 0.0)
    log_ref[...] = jnp.sum(logs, axis=0, keepdims=True)[:, :H]
    keep_log = pltpu.make_async_copy(log_ref, log_out, loc_sem.at[2])
    keep_log.start()

    for stage, like in enumerate((s1a, s1b, s2a, s2b, None, None, None, s2a, s2b, ps, None, None, lg)):
        if like is not None:
            both(stage, like.at[pl.ds(0, 7)]).wait_send()
    for stage, like in ((4, qg), (5, o_in), (6, st_in)):
        both(stage, like.at[pl.ds(0, OWN - 1)]).wait_send()
    for copy in kv_sent:
        copy.wait_send()
    keep_log.wait()
    keep_a.wait()
    keep_b.wait()
    both(10, s1a.at[pl.ds(0, 7)]).wait_send()
    both(11, s1b.at[pl.ds(0, 7)]).wait_send()
    both(11, s1b.at[pl.ds(0, 7)]).wait_recv()
    both(10, s1a.at[pl.ds(0, 7)]).wait_recv()


def body(queries, keys, values, query_host, lengths):
    bf16, f32 = jnp.bfloat16, jnp.float32
    attended, log_total = pl.pallas_call(
        kernel,
        out_shape=(
            jax.ShapeDtypeStruct((T, HD), bf16),
            jax.ShapeDtypeStruct((1, H), f32),
        ),
        in_specs=[
            pl.BlockSpec(memory_space=pl.ANY),
            pl.BlockSpec(memory_space=pl.ANY),
            pl.BlockSpec(memory_space=pl.ANY),
            pl.BlockSpec(memory_space=pl.ANY),
            pl.BlockSpec(memory_space=pl.ANY),
        ],
        out_specs=(
            pl.BlockSpec(memory_space=pl.ANY),
            pl.BlockSpec(memory_space=pl.ANY),
        ),
        scratch_shapes=[
            pltpu.SMEM((1,), jnp.int32),
            pltpu.SMEM((1, 1), jnp.int32),
            pltpu.VMEM((4, 2 * KEYS + 16, DH), bf16),
            pltpu.VMEM((NXY, T, 512), bf16),
            pltpu.VMEM((NZ, 16, 1024), bf16),
            pltpu.VMEM((NZ, 16, 256), bf16),
            pltpu.VMEM((NXY, 16, 128), bf16),
            pltpu.VMEM((NZ, 16, 256), bf16),
            pltpu.VMEM((NXY, 16, 128), bf16),
            pltpu.VMEM((OWN, 16, 384), bf16),
            pltpu.VMEM((4, ROWS, DH), bf16),
            pltpu.VMEM((4, ROWS, 2 * DH), f32),
            pltpu.VMEM((OWN, PIECE, DH), bf16),
            pltpu.VMEM((OWN, 1, DH), f32),
            pltpu.VMEM((OWN, PIECE, DH), bf16),
            pltpu.VMEM((OWN, 1, DH), f32),
            pltpu.VMEM((T, 512), bf16),
            pltpu.VMEM((16, 1024), bf16),
            pltpu.VMEM((NXY, NZ, 1, DH), f32),
            pltpu.VMEM((1, H), f32),
            pltpu.SemaphoreType.DMA((6,)),
            pltpu.SemaphoreType.DMA((3,)),
            pltpu.SemaphoreType.DMA((3,)),
            pltpu.SemaphoreType.DMA((13,)),
            pltpu.SemaphoreType.DMA((13,)),
        ],
        compiler_params=pltpu.CompilerParams(
            collective_id=0, has_side_effects=True, vmem_limit_bytes=40 * 2**20),
    )(
        query_host, lengths,
        pltpu.with_memory_space_constraint(queries.reshape(T, HD), pltpu.HBM),
        pltpu.with_memory_space_constraint(keys.reshape(KEYS, DH), pltpu.HBM),
        pltpu.with_memory_space_constraint(values.reshape(KEYS, DH), pltpu.HBM))
    return attended[None], log_total[None]


def solution(mesh):
    return jax.shard_map(
        body,
        mesh=mesh,
        in_specs=(
            P("req", "ctx", None, None),
            P("req", "ctx", None),
            P("req", "ctx", None),
            P("req"),
            P("req", "ctx"),
        ),
        out_specs=(P("req", None, None), P("req", "ctx", None)),
        check_vma=False,
    )
```

```python
import math

import jax
import jax.numpy as jnp
from jax import lax
from jax.experimental import pallas as pl
from jax.experimental.pallas import tpu as pltpu
from jax.sharding import PartitionSpec as P


H = 48
DH = 128
T = 64
KEYS = 512
BLOCK = 128
HD = H * DH
NZ = 8
NXY = 8
ROWS = 384
OWN = 16
PIECE = 48
A_COLS = 4096
NEG = -1e30
LOG2E = math.log2(math.e)
LN2 = math.log(2.0)
SCALE = DH ** -0.5 * LOG2E
MESH = pl.DeviceIdType.MESH


def kernel(host_in, len_in, q_ref, k_ref, v_ref, out_ref, log_out,
           host_ref, len_ref, kv, s1a, s1b, x2a, x2b, s2a, s2b, qg, qm, acc, po, ps, o_in, st_in,
           oa, ob, lg, log_ref, loc_sem, kv_send, kv_recv, send, recv):
    me = lax.axis_index("ctx")
    x, z, y = me // 32, (me // 4) % 8, me % 4
    xy = x * 4 + y
    tg, hg = z // 2, z % 2
    mine_kv, over_kv = x * 2 + y % 2, (1 - x) * 2 + y % 2

    def z_of(k):
        return lax.rem(z + k, NZ)

    def at_z(zz):
        return {"ctx": x * 32 + zz * 4 + y}

    def owner_to(k):
        zz = z_of(k % NZ)
        return zz + k // NZ * NZ, {"ctx": x * 32 + zz * 4 + (y if k < NZ else 3 - y)}

    def xy_to(k):
        px, py = lax.rem(x + k // 4, 2), lax.rem(y + k % 4, 4)
        return px * 4 + py, {"ctx": px * 32 + z * 4 + py}

    def put(src, dst, stage, device):
        pltpu.make_async_remote_copy(
            src_ref=src, dst_ref=dst, send_sem=send.at[stage], recv_sem=recv.at[stage],
            device_id=device, device_id_type=MESH).start()

    def both(stage, like):
        return pltpu.make_async_remote_copy(
            src_ref=like, dst_ref=like, send_sem=send.at[stage], recv_sem=recv.at[stage],
            device_id=at_z(z_of(1)), device_id_type=MESH)

    def cols(start, n):
        return pl.ds(pl.multiple_of(start, 128), n)

    def rows(start, n):
        return pl.ds(pl.multiple_of(start, 16), n)

    z_order = (4, 3, 5, 2, 6, 1, 7)
    xy_order = (6, 5, 7, 2, 4, 1, 3)
    owner_order = (12, 4, 11, 13, 3, 5, 10, 14, 2, 6, 9, 15, 1, 7, 8)

    def a_chunk(c):
        return q_ref.at[:, cols(c * 512, 512)]

    def b_chunk(zz):
        return q_ref.at[rows((zz // 2) * 16, 16), cols(A_COLS + lax.rem(zz, 2) * 1024, 1024)]

    barrier = pltpu.get_barrier_semaphore()
    for k in (4, 3, 5):
        pl.semaphore_signal(barrier, inc=1, device_id=at_z(z_of(k)), device_id_type=MESH)
    for k in (6, 5, 7):
        pl.semaphore_signal(barrier, inc=1, device_id=xy_to(k)[1], device_id_type=MESH)
    for k in ():
        pl.semaphore_signal(barrier, inc=1, device_id=owner_to(k)[1], device_id_type=MESH)
    for k in (2, 6):
        pl.semaphore_signal(barrier, inc=1, device_id=at_z(z_of(k)), device_id_type=MESH)
    for k in (2, 4, 1, 3):
        pl.semaphore_signal(barrier, inc=1, device_id=xy_to(k)[1], device_id_type=MESH)
    for k in ():
        pl.semaphore_signal(barrier, inc=1, device_id=owner_to(k)[1], device_id_type=MESH)
    for k in (1, 7):
        pl.semaphore_signal(barrier, inc=1, device_id=at_z(z_of(k)), device_id_type=MESH)
    for k in ():
        pl.semaphore_signal(barrier, inc=1, device_id=xy_to(k)[1], device_id_type=MESH)
    for k in ():
        pl.semaphore_signal(barrier, inc=1, device_id=owner_to(k)[1], device_id_type=MESH)
    local = [
        pltpu.make_async_copy(len_in, len_ref, loc_sem.at[4]),
        pltpu.make_async_copy(host_in, host_ref, loc_sem.at[5]),
        pltpu.make_async_copy(k_ref, kv.at[mine_kv, pl.ds(0, KEYS)], loc_sem.at[0]),
        pltpu.make_async_copy(v_ref, kv.at[mine_kv, pl.ds(KEYS, KEYS)], loc_sem.at[1]),
        pltpu.make_async_copy(a_chunk(xy), s1a.at[xy], loc_sem.at[2]),
        pltpu.make_async_copy(b_chunk(z), s1b.at[z], loc_sem.at[3]),
    ]
    for copy in local:
        copy.start()
    pl.semaphore_wait(barrier, 14)

    for k in xy_order:
        c, device = xy_to(k)
        put(a_chunk(c), s1a.at[xy], 0, device)
    for k in z_order:
        zz = z_of(k)
        put(b_chunk(zz), s1b.at[z], 1, at_z(zz))
    local[0].wait()
    length = len_ref[0, 0].astype(jnp.float32)
    kv[mine_kv, 2 * KEYS:, :] = jnp.full((16, DH), length, jnp.float32).astype(jnp.bfloat16)
    local[2].wait()
    local[3].wait()
    over = {"ctx": (1 - x) * 32 + z * 4 + y}
    pair = {"ctx": x * 32 + z * 4 + y + 1 - y % 2 * 2}

    def kv_copy(slot, sem, device):
        return pltpu.make_async_remote_copy(
            src_ref=kv.at[slot], dst_ref=kv.at[slot], send_sem=kv_send.at[sem], recv_sem=kv_recv.at[sem],
            device_id=device, device_id_type=MESH)

    kv_sent = [kv_copy(mine_kv, 0, over), kv_copy(mine_kv, 1, pair), kv_copy(over_kv, 2, pair)]
    kv_got = [
        kv_copy(over_kv, 0, over),
        kv_copy(x * 2 + 1 - y % 2, 1, pair),
        kv_copy((1 - x) * 2 + 1 - y % 2, 2, pair),
    ]
    kv_sent[0].start()
    kv_sent[1].start()

    local[1].wait()
    host = host_ref[0]
    host_z = lax.rem(host // 4, 8)
    host_xy = host // 32 * 4 + lax.rem(host, 4)
    local[4].wait()
    both(0, s1a.at[pl.ds(0, 7)]).wait_recv()
    chunk = s1a[host_xy]
    for p in range(NZ):
        a, b = p // 2, p % 2
        x2a[p] = chunk[16 * a:16 * a + 16, 256 * b:256 * b + 256]
    s2a[z] = x2a[z]
    for k in z_order:
        zz = z_of(k)
        put(x2a.at[zz], s2a.at[z], 2, at_z(zz))
    local[5].wait()
    both(1, s1b.at[pl.ds(0, 7)]).wait_recv()
    chunk = s1b[host_z]
    for p in range(NXY):
        x2b[p] = chunk[:, 128 * p:128 * p + 128]
    s2b[xy] = x2b[xy]
    for k in xy_order:
        c, device = xy_to(k)
        put(x2b.at[c], s2b.at[xy], 3, device)

    kv_got[0].wait_recv()
    kv_sent[2].start()

    both(2, s2a.at[pl.ds(0, 7)]).wait_recv()
    both(3, s2b.at[pl.ds(0, 7)]).wait_recv()
    qg[z, :, 0:256] = s2a[host_z]
    qg[z, :, 256:384] = s2b[host_xy]
    for k in owner_order:
        n, device = owner_to(k)
        put(qg.at[z], qg.at[z + k // NZ * NZ], 4, device)
    kv_got[1].wait_recv()
    kv_got[2].wait_recv()

    block_id = (lax.broadcasted_iota(jnp.int32, (1, KEYS), 1) // BLOCK).astype(jnp.float32)
    lane = lax.broadcasted_iota(jnp.int32, (PIECE, DH), 1)
    diagonal = lane == lax.broadcasted_iota(jnp.int32, (PIECE, DH), 0)
    valid = []
    for c in range(4):
        count = kv[c, 2 * KEYS:2 * KEYS + 16, :].astype(jnp.float32)[0:1, :]
        valid.append(block_id < jnp.concatenate([count] * (KEYS // DH), axis=1))
    both(4, qg.at[pl.ds(0, OWN - 1)]).wait_recv()

    def attend(group, ks):
        targets = [owner_to(k) for k in ks]
        size = PIECE * len(ks)
        for i, (n, _) in enumerate(targets):
            for c in range(3):
                qm[group, PIECE * i + 16 * c:PIECE * i + 16 * c + 16, :] = qg[n, :, 128 * c:128 * c + 128]
        old = total = None
        for c in range(4):
            score = lax.dot_general(
                qm[group, 0:size, :], kv[c, 0:KEYS, :], (((1,), (1,)), ((), ())),
                preferred_element_type=jnp.float32)
            score = jnp.where(valid[c], score * SCALE, NEG)
            new = jnp.max(score, axis=1, keepdims=True)
            if c:
                new = jnp.maximum(old, new)
            weight = jnp.exp2(score - new).astype(jnp.bfloat16)
            value = jnp.concatenate(
                [kv[c, KEYS:2 * KEYS, :], jnp.ones((KEYS, DH), jnp.bfloat16)], axis=1)
            summed = jnp.dot(weight, value, preferred_element_type=jnp.float32)
            acc[group, 0:size, :] = acc[group, 0:size, :] * jnp.exp2(old - new) + summed if c else summed
            old = new
        total = acc[group, 0:size, DH:]
        part = (acc[group, 0:size, :DH] / total).astype(jnp.bfloat16)
        lse = old + jnp.log(total) * LOG2E
        for i, (k, (n, device)) in enumerate(zip(ks, targets)):
            at = slice(PIECE * i, PIECE * i + PIECE)
            stat = jnp.sum(jnp.where(diagonal, lse[at, :], 0.0), axis=0, keepdims=True)
            if k:
                po[n], ps[n] = part[at, :], stat
                put(po.at[n], o_in.at[k // NZ * NZ + z], 5, device)
                put(ps.at[n], st_in.at[k // NZ * NZ + z], 6, device)
            else:
                o_in[z], st_in[z] = part[at, :], stat

    for group, ks in enumerate(((12, 11, 13, 4), (10, 14, 3, 5), (9, 15, 2, 6), (8, 1, 7, 0))):
        attend(group, ks)
    both(6, st_in.at[pl.ds(0, OWN - 1)]).wait_recv()
    stat = jnp.concatenate([st_in[s] for s in range(OWN)], axis=0)
    overall = jnp.max(stat, axis=0, keepdims=True)
    share = jnp.exp2(stat - overall)
    summed = jnp.sum(share, axis=0, keepdims=True)
    share = share / summed
    lg[xy, z] = overall * LN2 + jnp.log(summed)
    for k in z_order:
        put(lg.at[xy, z], lg.at[xy, z], 9, at_z(z_of(k)))
    both(5, o_in.at[pl.ds(0, OWN - 1)]).wait_recv()
    result = jnp.zeros((PIECE, DH), jnp.float32)
    for s in range(OWN):
        column = jnp.sum(jnp.where(diagonal, share[s:s + 1, :], 0.0), axis=1, keepdims=True)
        result = result + column * o_in[s].astype(jnp.float32)
    result = result.astype(jnp.bfloat16)

    mine = rows(tg * 16, 16)
    oa_mine = oa.at[mine, cols(hg * 256, 256)]
    ob_mine = ob.at[:, cols(xy * 128, 128)]
    oa[mine, cols(hg * 256, 128)] = result[0:16]
    oa[mine, cols(hg * 256 + 128, 128)] = result[16:32]
    ob[:, cols(xy * 128, 128)] = result[32:48]
    for k in z_order:
        put(oa_mine, oa_mine, 7, at_z(z_of(k)))
    for k in xy_order:
        put(ob_mine, ob_mine, 8, xy_to(k)[1])
    both(9, ps.at[pl.ds(0, 7)]).wait_recv()
    for k in xy_order:
        put(lg.at[xy], lg.at[xy], 12, xy_to(k)[1])
    a_out = out_ref.at[:, cols(xy * 512, 512)]
    b_out = out_ref.at[mine, cols(A_COLS + hg * 1024, 1024)]
    both(7, s2a.at[pl.ds(0, 7)]).wait_recv()
    for k in xy_order:
        put(oa, a_out, 10, xy_to(k)[1])
    keep_a = pltpu.make_async_copy(oa, a_out, loc_sem.at[0])
    keep_a.start()
    both(8, s2b.at[pl.ds(0, 7)]).wait_recv()
    for k in z_order:
        put(ob, b_out, 11, at_z(z_of(k)))
    keep_b = pltpu.make_async_copy(ob, b_out, loc_sem.at[1])
    keep_b.start()

    both(12, lg.at[pl.ds(0, 7)]).wait_recv()
    t_group, t_in = me // 16, lax.rem(me, 16)
    lane = lax.broadcasted_iota(jnp.int32, (NXY, DH), 1)
    source = lax.broadcasted_iota(jnp.int32, (NXY, DH), 0)
    logs = jnp.zeros((NXY, DH), jnp.float32)
    for b in range(2):
        part = jnp.concatenate([lg[c, 2 * t_group + b] for c in range(NXY)], axis=0)
        for c in range(3):
            column = jnp.sum(jnp.where(lane == 16 * c + t_in, part, 0.0), axis=1, keepdims=True)
            head = source * 4 + 2 * b + c if c < 2 else 32 + 8 * b + source
            logs = logs + jnp.where(lane == head, column, 0.0)
    log_ref[...] = jnp.sum(logs, axis=0, keepdims=True)[:, :H]
    keep_log = pltpu.make_async_copy(log_ref, log_out, loc_sem.at[2])
    keep_log.start()

    for stage, like in enumerate((s1a, s1b, s2a, s2b, None, None, None, s2a, s2b, ps, None, None, lg)):
        if like is not None:
            both(stage, like.at[pl.ds(0, 7)]).wait_send()
    for stage, like in ((4, qg), (5, o_in), (6, st_in)):
        both(stage, like.at[pl.ds(0, OWN - 1)]).wait_send()
    for copy in kv_sent:
        copy.wait_send()
    keep_log.wait()
    keep_a.wait()
    keep_b.wait()
    both(10, s1a.at[pl.ds(0, 7)]).wait_send()
    both(11, s1b.at[pl.ds(0, 7)]).wait_send()
    both(11, s1b.at[pl.ds(0, 7)]).wait_recv()
    both(10, s1a.at[pl.ds(0, 7)]).wait_recv()


def body(queries, keys, values, query_host, lengths):
    bf16, f32 = jnp.bfloat16, jnp.float32
    attended, log_total = pl.pallas_call(
        kernel,
        out_shape=(
            jax.ShapeDtypeStruct((T, HD), bf16),
            jax.ShapeDtypeStruct((1, H), f32),
        ),
        in_specs=[
            pl.BlockSpec(memory_space=pl.ANY),
            pl.BlockSpec(memory_space=pl.ANY),
            pl.BlockSpec(memory_space=pl.ANY),
            pl.BlockSpec(memory_space=pl.ANY),
            pl.BlockSpec(memory_space=pl.ANY),
        ],
        out_specs=(
            pl.BlockSpec(memory_space=pl.ANY),
            pl.BlockSpec(memory_space=pl.ANY),
        ),
        scratch_shapes=[
            pltpu.SMEM((1,), jnp.int32),
            pltpu.SMEM((1, 1), jnp.int32),
            pltpu.VMEM((4, 2 * KEYS + 16, DH), bf16),
            pltpu.VMEM((NXY, T, 512), bf16),
            pltpu.VMEM((NZ, 16, 1024), bf16),
            pltpu.VMEM((NZ, 16, 256), bf16),
            pltpu.VMEM((NXY, 16, 128), bf16),
            pltpu.VMEM((NZ, 16, 256), bf16),
            pltpu.VMEM((NXY, 16, 128), bf16),
            pltpu.VMEM((OWN, 16, 384), bf16),
            pltpu.VMEM((4, ROWS, DH), bf16),
            pltpu.VMEM((4, ROWS, 2 * DH), f32),
            pltpu.VMEM((OWN, PIECE, DH), bf16),
            pltpu.VMEM((OWN, 1, DH), f32),
            pltpu.VMEM((OWN, PIECE, DH), bf16),
            pltpu.VMEM((OWN, 1, DH), f32),
            pltpu.VMEM((T, 512), bf16),
            pltpu.VMEM((16, 1024), bf16),
            pltpu.VMEM((NXY, NZ, 1, DH), f32),
            pltpu.VMEM((1, H), f32),
            pltpu.SemaphoreType.DMA((6,)),
            pltpu.SemaphoreType.DMA((3,)),
            pltpu.SemaphoreType.DMA((3,)),
            pltpu.SemaphoreType.DMA((13,)),
            pltpu.SemaphoreType.DMA((13,)),
        ],
        compiler_params=pltpu.CompilerParams(
            collective_id=0, has_side_effects=True, vmem_limit_bytes=40 * 2**20),
    )(
        query_host, lengths,
        pltpu.with_memory_space_constraint(queries.reshape(T, HD), pltpu.HBM),
        pltpu.with_memory_space_constraint(keys.reshape(KEYS, DH), pltpu.HBM),
        pltpu.with_memory_space_constraint(values.reshape(KEYS, DH), pltpu.HBM))
    return attended[None], log_total[None]


def solution(mesh):
    return jax.shard_map(
        body,
        mesh=mesh,
        in_specs=(
            P("req", "ctx", None, None),
            P("req", "ctx", None),
            P("req", "ctx", None),
            P("req"),
            P("req", "ctx"),
        ),
        out_specs=(P("req", None, None), P("req", "ctx", None)),
        check_vma=False,
    )
```
